128 devices in a mesh: lon: 32 (over y, z, x_lo), lat: 4 (over x_hi, core).
Axes of the slice: x: 4 (x_hi: 2, x_lo: 2; x = x_hi * 2 + x_lo), y: 4, z: 4, core: 2. Of those that a mesh axis runs over, the one named last changes fastest.
Arguments:
- latent_state: bfloat16 [512, 64, 512], P('lon', 'lat'), may hold values from -6 to 6
- cotangent: bfloat16 [512, 64, 512], P('lon', 'lat'), may hold values from -6 to 6
- w_inner: bfloat16 [512, 1024], replicated, may hold values from -0.25 to 0.25
- w_outer: bfloat16 [1024, 512], replicated, may hold values from -0.1875 to 0.1875
- norm_gain: float32 [512], replicated, may hold values from 0.5 to 1.5
- source_block: int32 [512, 64], P('lon', 'lat'), may hold values from 0 to 127, as said below
- corner_code: int32 [512, 64], P('lon', 'lat'), may hold values from 0 to 54, as said below
- frac_lon: float32 [512, 64], P('lon', 'lat'), may hold values from 0 to 1
- frac_lat: float32 [512, 64], P('lon', 'lat'), may hold values from 0 to 1
- terrain: int32 [512, 64], P('lon', 'lat'), may hold values from 0 to 7
- kappa_table: float32 [8], replicated, may hold values from 0.05 to 0.24
Outputs:
- state_out: bfloat16 [512, 64, 512], P('lon', 'lat')
- state_grad: bfloat16 [512, 64, 512], P('lon', 'lat')
- grad_inner: float32 [512, 1024], replicated
- grad_outer: float32 [1024, 512], replicated
- grad_gain: float32 [512], replicated
The draws below stay inside these ranges and needn't reach their ends.
Inputs may be any that keep to these rules, and one draw needn't show every extreme that they name: `source_block`: the block's latitude part lies in the target's own lat tile; values run over all 8 x 8 blocks of that tile row. Row corner_code // 8 and column corner_code % 8 are both at most 6.
All inputs are finite; a program needn't handle non-finite values.
Results may differ from the reference program's by a relative error of at most 0.017.
Values may be sent and summed in bfloat16 or wider, within the bound.
A program may use at most 128 MiB of HBM per device.

```python
import jax
import jax.numpy as jnp
from jax import lax

C = 512
HID = 1024
STEPS = 4
NCLASS = 8
TLAT = 16
NLON = 512
NLAT = 64


def draw_source_block(key, part):
    blocks = NLON // 8
    tiles = NLAT // TLAT
    per_row = TLAT // 8
    lon_cell = jnp.arange(NLON, dtype=jnp.int32)[:, None]
    lat_cell = jnp.arange(NLAT, dtype=jnp.int32)[None, :]
    distance = jnp.abs(2 * (lat_cell // TLAT) + 1 - tiles)
    reach = 1 + (blocks // 2 - 1) * distance // max(tiles - 1, 1)
    reach = jnp.broadcast_to(reach, (NLON, NLAT))
    first_key = jax.random.fold_in(key, 11)
    second_key = jax.random.fold_in(key, 12)
    third_key = jax.random.fold_in(key, 13)
    fourth_key = jax.random.fold_in(key, 14)
    offset = jax.random.randint(first_key, (NLON, NLAT), -reach, reach + 1)
    far_pick = jax.random.randint(third_key, (NLON, NLAT), 0, 4) == 0
    far_offset = jax.random.randint(fourth_key, (NLON, NLAT), -(blocks // 2), blocks // 2 + 1)
    offset = jnp.where(far_pick, far_offset, offset)
    polar = jnp.broadcast_to(distance == tiles - 1, (NLON, NLAT))
    marked = jnp.logical_and(lon_cell % 8 == 0, lat_cell % TLAT == 0)
    offset = jnp.where(jnp.logical_and(polar, marked), blocks // 2, offset)
    lon_block = (lon_cell // 8 + offset) % blocks
    lat_block = jax.random.randint(second_key, (NLON, NLAT), 0, per_row)
    return (lon_block * per_row + lat_block).astype(jnp.int32)


def draw_corner_code(key, part):
    first_key = jax.random.fold_in(key, 21)
    second_key = jax.random.fold_in(key, 22)
    row_part = jax.random.randint(first_key, (NLON, NLAT), 0, 7)
    col_part = jax.random.randint(second_key, (NLON, NLAT), 0, 7)
    return (row_part * 8 + col_part).astype(jnp.int32)


def place_ends(result, own_key, low, top_value):
    longest = result.shape.index(max(result.shape))
    spots = []
    for shift in (0, 1):
        where = [jax.random.randint(jax.random.fold_in(own_key, axis), (), 0, length) for axis, length in enumerate(result.shape)]
        where[longest] = (where[longest] + shift) % result.shape[longest]
        spots.append(tuple(where))
    return result.at[spots[0]].set(low).at[spots[1]].set(top_value)


def block_scale(stream_key, shape, cuts, low, high):
    level = 1.0
    for axis_at, blocks in cuts:
        heights = jax.random.uniform(jax.random.fold_in(jax.random.fold_in(stream_key, 6), axis_at), (blocks,), jnp.float32, low / len(cuts), high / len(cuts))
        level = level * jnp.repeat(jnp.exp(heights), shape[axis_at] // blocks).reshape((-1,) + (1,) * (len(shape) - 1 - axis_at))
    return level


def centred(own_key, dims, scale, most, cuts=(), held_as=jnp.bfloat16):
    array = jax.random.normal(own_key, dims, jnp.float32) * scale
    if len(cuts) > 0:
        array = block_scale(own_key, dims, cuts, -0.22, 0.18) * array
    return jnp.clip(array, min=-most, max=most).astype(held_as)


def setup_inputs(seed: int = 0) -> dict:
    key_list = jax.random.split(jax.random.key(seed), 12)
    return {
        "latent_state": centred(key_list[0], (NLON, NLAT, C), 1.0, 6.0, ((0, 32), (1, 4))),
        "cotangent": centred(key_list[1], (NLON, NLAT, C), 1.0, 6.0, ((0, 32), (1, 4))),
        "w_inner": centred(key_list[2], (C, HID), C ** -0.5, 0.25),
        "w_outer": centred(key_list[3], (HID, C), HID ** -0.5, 0.1875),
        "norm_gain": jnp.clip(1.0 + 0.1 * jax.random.normal(key_list[4], (C,), jnp.float32), 0.5, 1.5),
        "source_block": draw_source_block(jax.random.fold_in(key_list[11], 71), 0),
        "corner_code": draw_corner_code(jax.random.fold_in(key_list[11], 71), 0),
        "frac_lon": jnp.clip(1.0 * jax.random.uniform(key_list[7], (NLON, NLAT), jnp.float32) ** block_scale(key_list[7], (NLON, NLAT), ((0, 32), (1, 4)), -0.2, 0.2), 0.0, 1.0),
        "frac_lat": jnp.clip(1.0 * jax.random.uniform(key_list[8], (NLON, NLAT), jnp.float32) ** block_scale(key_list[8], (NLON, NLAT), ((0, 32), (1, 4)), -0.2, 0.2), 0.0, 1.0),
        "terrain": place_ends(jax.random.randint(key_list[9], (NLON, NLAT), 0, NCLASS), jax.random.fold_in(key_list[9], 1), 0, NCLASS - 1).astype(jnp.int32),
        "kappa_table": jnp.clip(jax.random.uniform(key_list[10], (NCLASS,), jnp.float32, 0.05, 0.24), 0.05, 0.24),
    }


def source_cells(source_block, corner_code):
    per_row = TLAT // 8
    lat_tile = (jnp.arange(NLAT, dtype=jnp.int32) // TLAT)[None, :]
    lon_source = source_block // per_row * 8 + corner_code // 8
    lat_source = lat_tile * TLAT + source_block % per_row * 8 + corner_code % 8
    return (lon_source.astype(jnp.int32), lat_source.astype(jnp.int32))

def laplace(field):
    rolled = jnp.roll(field, 1, 0) + jnp.roll(field, -1, 0)
    padded = jnp.pad(field, ((0, 0), (1, 1), (0, 0)))
    return rolled + padded[:, 2:] + padded[:, :-2] - 4.0 * field

def reference(latent_state, cotangent, w_inner, w_outer, norm_gain, source_block, corner_code, frac_lon, frac_lat, terrain, kappa_table):
    lon_source, lat_source = source_cells(source_block, corner_code)
    shifts = [(0, 0), (1, 0), (0, 1), (1, 1)]
    weights = [(1.0 - frac_lon) * (1.0 - frac_lat), frac_lon * (1.0 - frac_lat), (1.0 - frac_lon) * frac_lat, frac_lon * frac_lat]
    drift = jnp.zeros((NLON, NLAT, C), jnp.float32)
    for shift, weight in zip(shifts, weights):
        picked = latent_state[lon_source + shift[0], lat_source + shift[1]].astype(jnp.float32)
        drift = drift + weight[..., None] * picked
    kappa = kappa_table[terrain][..., None]
    field = drift
    for turn_index in range(STEPS):
        field = field + kappa * laplace(field)
    flat_field = field.reshape(NLON * NLAT, C)
    rstd = lax.rsqrt(lax.optimization_barrier(jnp.mean(flat_field * flat_field, -1, keepdims=True)) + 1e-06)
    normed = flat_field * rstd
    z_in = (normed * norm_gain).astype(jnp.bfloat16)
    pre_act = jnp.dot(z_in, w_inner, preferred_element_type=jnp.float32)
    act = jax.nn.silu(pre_act).astype(jnp.bfloat16)
    react = jnp.dot(act, w_outer, preferred_element_type=jnp.float32)
    state_out = (flat_field + react).astype(jnp.bfloat16).reshape(NLON, NLAT, C)
    cot = cotangent.reshape(NLON * NLAT, C)
    grad_outer = jnp.dot(act.T, cot, preferred_element_type=jnp.float32)
    grad_act = jnp.dot(cot, w_outer.T, preferred_element_type=jnp.float32)
    sigma = jax.nn.sigmoid(pre_act)
    grad_pre = (grad_act * sigma * (1.0 + pre_act * (1.0 - sigma))).astype(jnp.bfloat16)
    grad_inner = jnp.dot(z_in.T, grad_pre, preferred_element_type=jnp.float32)
    grad_z = jnp.dot(grad_pre, w_inner.T, preferred_element_type=jnp.float32)
    grad_gain = lax.optimization_barrier(jnp.sum(grad_z * normed, 0))
    grad_norm = grad_z * norm_gain
    grad_field = cot.astype(jnp.float32) + rstd * (grad_norm - normed * lax.optimization_barrier(jnp.mean(grad_norm * normed, -1, keepdims=True)))
    grad_field = grad_field.reshape(NLON, NLAT, C)
    for turn_index in range(STEPS):
        grad_field = grad_field + laplace(kappa * grad_field)
    grad_drift = grad_field.astype(jnp.bfloat16).astype(jnp.float32)
    total = jnp.zeros((NLON, NLAT, C), jnp.float32)
    for shift, weight in zip(shifts, weights):
        part = (weight[..., None] * grad_drift).astype(jnp.bfloat16).astype(jnp.float32)
        total = total.at[lon_source + shift[0], lat_source + shift[1]].add(part)
    return (state_out, total.astype(jnp.bfloat16), grad_inner, grad_outer, grad_gain)
```

```python
import functools

import jax
import jax.numpy as jnp
import numpy as np
from jax import lax
from jax.experimental import pallas as pl
from jax.experimental.pallas import tpu as pltpu
from jax.sharding import PartitionSpec as P

MESH = pl.DeviceIdType.MESH
F32 = jnp.float32
BF16 = jnp.bfloat16
NL = 32
NT = 4
CELLS = 256
CH = 512
HID = 1024
SLOT = 64
NS = NL * SLOT
PAIRS = NL // 2
NEAR_PAIRS = 6
CAP_NEAR = 48
CAP_FAR = 32
BACK = 5
EXT = 640
NEIGH = ((-1, 0), (1, 0), (0, -1), (0, 1), (-1, -1), (-1, 1), (1, -1), (1, 1))


def ext_cells():
    cells = [(x, y) for x in range(16) for y in range(16)]
    low, mid, top = range(-4, 0), range(16), range(16, 20)
    for dx, dy in NEIGH:
        xs = (low, mid, top)[dx + 1]
        ys = (low, mid, top)[dy + 1]
        cells += [(x, y) for x in xs for y in ys]
    return np.array(cells)


def tables():
    cells = ext_cells()
    count = len(cells)
    dist = np.abs(cells[:, None] - cells[None, :]).sum(-1)
    adj = np.zeros((EXT, EXT), np.float32)
    adj[:count, :count] = dist == 1
    ys = np.full((EXT,), -1000.0, np.float32)
    ys[:count] = cells[:, 1]
    ycol = np.broadcast_to(ys[:, None], (EXT, 128))
    yrow = np.broadcast_to(ys[None, :], (8, EXT))
    sel = np.zeros((384, CELLS), np.float32)
    at = 0
    for dx, dy in NEIGH:
        width = (4 if dx else 16) * (4 if dy else 16)
        for q in range(width):
            x, y = cells[256 + at + q]
            sel[at + q, (x - 16 * dx) * 16 + (y - 16 * dy)] = 1.0
        at += width
    spread = (np.arange(256)[None, :] % 16 == np.arange(16)[:, None]).astype(np.float32)
    return adj, ycol, yrow, sel, spread


def nn(a, b):
    return jnp.dot(a, b, preferred_element_type=F32)


def nt(a, b):
    return lax.dot_general(a, b, (((1,), (1,)), ((), ())), preferred_element_type=F32)


def tn(a, b):
    return lax.dot_general(a, b, (((0,), (0,)), ((), ())), preferred_element_type=F32)


def split2(v):
    hi = v.astype(BF16)
    return hi, (v - hi.astype(F32)).astype(BF16)


def iota(shape, dim):
    return lax.broadcasted_iota(jnp.int32, shape, dim).astype(F32)

STEPS = 4


def with_halo(value, sides, width, wrap):
    for axis, dim in sides:
        size, length = (lax.axis_size(axis), value.shape[dim])
        up = [(i, (i + 1) % size) for i in range(size if wrap else size - 1)]
        down = [(j, i) for i, j in up]
        last = lax.slice_in_dim(value, length - width, length, axis=dim)
        first = lax.slice_in_dim(value, 0, width, axis=dim)
        before = lax.ppermute(last, axis, up)
        after = lax.ppermute(first, axis, down)
        value = jnp.concatenate([before, value, after], axis=dim)
    return value


def flat_sources(source_block, corner_code, lat_cells):
    per_row = lat_cells // 8
    lon_part = source_block // per_row * 8 + corner_code // 8
    lat_part = source_block % per_row * 8 + corner_code % 8
    return lon_part * lat_cells + lat_part


def corner_table(flat_ids, frac_a, frac_b, lat_cells):
    shifted = jnp.stack([flat_ids, flat_ids + lat_cells, flat_ids + 1, flat_ids + lat_cells + 1])
    weights = jnp.stack(
        [
            (1.0 - frac_a) * (1.0 - frac_b),
            frac_a * (1.0 - frac_b),
            (1.0 - frac_a) * frac_b,
            frac_a * frac_b,
        ]
    )
    return (shifted, weights)


def laplace(field):
    wide = with_halo(field.astype(jnp.bfloat16), (("lon", 0),), 1, True).astype(field.dtype)
    tall = with_halo(field.astype(jnp.bfloat16), (("lat", 1),), 1, False).astype(field.dtype)
    return wide[2:] + wide[:-2] + tall[:, 2:] + tall[:, :-2] - 4.0 * field


def on_device_general(
    latent_state,
    cotangent,
    w_inner,
    w_outer,
    norm_gain,
    source_block,
    corner_code,
    frac_lon,
    frac_lat,
    terrain,
    kappa_table,
):
    lon_cells, lat_cells, chans = latent_state.shape
    cells = lon_cells * lat_cells
    flat_ids = flat_sources(source_block, corner_code, lat_cells)
    shifted, weights = corner_table(
        flat_ids.reshape(cells), frac_lon.reshape(cells), frac_lat.reshape(cells), lat_cells
    )
    shard_piece = lax.all_gather(latent_state, "lon", axis=0, tiled=True)
    count = shard_piece.shape[0] * lat_cells
    local = shifted
    hits = local[:, :, None] == jnp.arange(count, dtype=jnp.int32)[None, None, :]
    select = jnp.sum(jnp.where(hits, weights[:, :, None], 0.0), 0)
    upper = select.astype(jnp.bfloat16)
    lower = (select - upper.astype(jnp.float32)).astype(jnp.bfloat16)
    values = shard_piece.reshape(count, chans)
    running = jnp.dot(upper, values, preferred_element_type=jnp.float32)
    drift = running + jnp.dot(lower, values, preferred_element_type=jnp.float32)
    drift = drift.reshape(lon_cells, lat_cells, chans)
    classes = jnp.arange(kappa_table.shape[0], dtype=jnp.int32)
    kappa = jnp.sum(jnp.where(terrain[..., None] == classes, kappa_table, 0.0), -1)[..., None]
    field = drift
    for turn_index in range(STEPS):
        field = field + kappa * laplace(field)
    flat_field = field.reshape(cells, chans)
    rstd = lax.rsqrt(jnp.mean(flat_field * flat_field, -1, keepdims=True) + 1e-06)
    normed = flat_field * rstd
    z_in = (normed * norm_gain).astype(jnp.bfloat16)
    pre_act = jnp.dot(z_in, w_inner, preferred_element_type=jnp.float32)
    act = jax.nn.silu(pre_act).astype(jnp.bfloat16)
    react = jnp.dot(act, w_outer, preferred_element_type=jnp.float32)
    state_out = (flat_field + react).astype(jnp.bfloat16).reshape(lon_cells, lat_cells, chans)
    cot = cotangent.reshape(cells, chans)
    local_outer = jnp.dot(act.T, cot, preferred_element_type=jnp.float32)
    grad_act = jnp.dot(cot, w_outer.T, preferred_element_type=jnp.float32)
    sigma = jax.nn.sigmoid(pre_act)
    grad_pre = (grad_act * sigma * (1.0 + pre_act * (1.0 - sigma))).astype(jnp.bfloat16)
    local_inner = jnp.dot(z_in.T, grad_pre, preferred_element_type=jnp.float32)
    grad_z = jnp.dot(grad_pre, w_inner.T, preferred_element_type=jnp.float32)
    local_gain = jnp.sum(grad_z * normed, 0)
    grad_norm = grad_z * norm_gain
    grad_field = cot.astype(jnp.float32) + rstd * (
        grad_norm - normed * jnp.mean(grad_norm * normed, -1, keepdims=True)
    )
    grad_field = grad_field.reshape(lon_cells, lat_cells, chans)
    for turn_index in range(STEPS):
        grad_field = grad_field + laplace(kappa * grad_field)
    grad_drift = grad_field.astype(jnp.bfloat16)
    parts = (weights[:, :, None] * grad_drift.reshape(cells, chans).astype(jnp.float32)).astype(
        jnp.bfloat16
    )
    count = lon_cells * lax.axis_size("lon")
    width = count * lat_cells
    local = shifted
    onehot = (local[:, :, None] == jnp.arange(width, dtype=jnp.int32)[None, None, :]).astype(
        jnp.bfloat16
    )
    term = jnp.einsum("ksr,ksc->rc", onehot, parts, preferred_element_type=jnp.float32)
    summed = lax.psum_scatter(
        term.reshape(count, lat_cells, chans).astype(jnp.bfloat16),
        "lon",
        scatter_dimension=0,
        tiled=True,
    )
    grad_inner, grad_outer, grad_gain = lax.psum(
        (local_inner, local_outer, local_gain), ("lon", "lat")
    )
    return (state_out, summed, grad_inner, grad_outer, grad_gain)


def kernel(
    lat_state, cot_ref, w_in, w_out, gain_ref, sb_ref, cc_ref, fa_ref, fb_ref, ter_ref, ktab,
    adj_ref, ycol_ref, yrow_ref, sel_ref, spread_ref,
    out_ref, grad_ref, gout, vec_ref,
    G, W_hi, W_lo, rows_out, rows_in, gro, gin, req_out, req_in, t_out, t_in,
    ext_f, ext_b, stage_f, stage_b, gd_ref, Mh, Ml, M2h, M2l, Ah, Al, Bh, Bl,
    z_ref, act_ref, gp_ref, gbuf, sib_in, hsum, rs_in, xh_out, xh_in, v_out, v_lat, v_sum, v_lon,
    s_req, r_req, s_row, r_row, s_gro, r_gro, s_ter, r_ter, s_hf, r_hf, s_hb, r_hb,
    s_sib, r_sib, s_rs, r_rs, s_xh, r_xh, s_ag, r_ag, s_fin, r_fin, s_vl, r_vl, s_vn, r_vn,
):
    me = lax.axis_index("lon")
    la = lax.axis_index("lat")
    core = lax.rem(la, 2)
    sib = la + 1 - 2 * core
    opp = lax.rem(la + 2, NT)

    def lon_at(d):
        return lax.rem(me + d + 2 * NL, NL)

    def lat_at(d):
        return lax.rem(la + d + NT, NT)

    def send(src, dst, ssem, rsem, lon, lat):
        return pltpu.make_async_remote_copy(
            src_ref=src, dst_ref=dst, send_sem=ssem, recv_sem=rsem,
            device_id=(lon, lat), device_id_type=MESH,
        )

    rows_in[...] = jnp.zeros((NS, CH), BF16)
    gin[...] = jnp.zeros((NS, CH), BF16)
    ext_f[576:EXT, :] = jnp.zeros((EXT - 576, CH), BF16)
    ext_b[576:EXT, :] = jnp.zeros((EXT - 576, CH), BF16)

    barrier = pltpu.get_barrier_semaphore()

    def greet(d, carry):
        pl.semaphore_signal(barrier, inc=1, device_id=(lon_at(d), la), device_id_type=MESH)
        return carry

    lax.fori_loop(1, NL, greet, 0)
    for dx, dy in NEIGH[2:]:
        pl.semaphore_signal(
            barrier, inc=1, device_id=(lon_at(dx), lat_at(dy)), device_id_type=MESH
        )
    pl.semaphore_signal(barrier, inc=1, device_id=(me, opp), device_id_type=MESH)

    raw = jnp.concatenate(
        [
            sb_ref[...].astype(F32), cc_ref[...].astype(F32), fa_ref[...], fb_ref[...],
            ter_ref[...].astype(F32),
        ],
        axis=0,
    )
    flat = jnp.dot(
        raw, spread_ref[...], precision=lax.Precision.HIGHEST, preferred_element_type=F32
    )
    own = jnp.floor(iota((16, CELLS), 1) * (1.0 / 16.0)) == iota((16, CELLS), 0)

    def line(k):
        return jnp.sum(jnp.where(own, flat[16 * k : 16 * k + 16], 0.0), 0, keepdims=True)

    sb, cc, fa, fb, ter = (line(k) for k in range(5))
    dev = jnp.floor(sb * 0.25)
    blon = jnp.floor(sb * 0.5)
    klon = jnp.floor(cc * 0.125)
    cell = ((blon - 2.0 * dev) * 8.0 + klon) * 16.0 + (sb - 2.0 * blon) * 8.0 + (cc - 8.0 * klon)
    slot = dev - me.astype(F32) + float(BACK)
    slot = jnp.where(slot < 0.0, slot + float(NL), slot)
    slot = jnp.where(slot >= float(NL), slot - float(NL), slot)
    hits = iota((NL, CELLS), 0) == slot
    before = (iota((CELLS, CELLS), 0) < iota((CELLS, CELLS), 1)).astype(F32).astype(BF16)
    counts = nn(jnp.where(hits, 1.0, 0.0).astype(BF16), before)
    rank = jnp.sum(jnp.where(hits, counts, 0.0), 0, keepdims=True)
    cap = jnp.where(slot < 2.0 * NEAR_PAIRS, float(CAP_NEAR), float(CAP_FAR))
    fits = rank < cap
    place = jnp.where(fits, slot * float(SLOT) + rank, -1.0)
    over = jnp.sum(jnp.where(fits, 0.0, 1.0), axis=1, keepdims=True)

    def fill_g(q, carry):
        row = pl.multiple_of(q * 128, 128)
        at = iota((128, CELLS), 0) + lax.convert_element_type(row, F32)
        G[pl.ds(row, 128), :] = jnp.where(at == place, 1.0, 0.0).astype(BF16)
        return carry

    lax.fori_loop(0, PAIRS, fill_g, 0)

    def rows_of(lines, height, width):
        which = iota((height, width), 0)
        out = jnp.zeros((height, width), F32)
        for k, v in enumerate(lines):
            out = out + jnp.where(which == float(k), v, 0.0)
        return out

    fah = fa.astype(BF16).astype(F32)
    fam = (fa - fah).astype(BF16).astype(F32)
    fbh = fb.astype(BF16).astype(F32)
    fbm = (fb - fbh).astype(BF16).astype(F32)
    params = rows_of(
        [cell, fah, fam, fa - fah - fam, fbh, fbm, fb - fbh - fbm, jnp.ones_like(fa)], 16, CELLS
    ).astype(BF16)
    for p in range(PAIRS):
        req_out[p] = nt(params, G[128 * p : 128 * p + 128, :])[0:8]
    t_all = nt(jnp.broadcast_to(ter, (16, CELLS)).astype(BF16), sel_ref[...])
    for q in range(3):
        t_out[q] = t_all[0:8, 128 * q : 128 * q + 128]

    pl.semaphore_wait(barrier, NL - 1 + 7)

    def req_copy(j):
        return send(
            req_out.at[j // 2], req_in.at[j], s_req.at[j], r_req.at[j], lon_at(j - BACK), la
        )

    def each_pair(body):
        def step(j, carry):
            @pl.when(j != BACK)
            def _():
                body(j)

            return carry

        lax.fori_loop(0, NL, step, 0)

    each_pair(lambda j: req_copy(j).start())

    def ter_copy(n):
        dx, dy = NEIGH[n]
        tile = (0, 0, 1, 1, 2, 2, 2, 2)[n]
        return send(
            t_out.at[tile], t_in.at[n], s_ter.at[n], r_ter.at[n], lon_at(-dx), lat_at(-dy)
        )

    for n in range(8):
        ter_copy(n).start()
    req_in[BACK] = req_out[BACK // 2]

    each_pair(lambda j: req_copy(j).wait_recv())
    lane_low = iota((8, 128), 1) < float(SLOT)

    def row_copy(j, cap_j):
        at = pl.multiple_of(j * SLOT, SLOT)
        return send(
            rows_out.at[pl.ds(at, cap_j), :], rows_in.at[pl.ds(at, cap_j), :],
            s_row.at[j], r_row.at[j], lon_at(BACK - j), la,
        )

    def make_rows(cap_j):
        def body(p, carry):
            t = jnp.where(lane_low, req_in[2 * p], req_in[2 * p + 1])
            cid = t[0:1]
            a = t[1:2] + t[2:3] + t[3:4]
            b = t[4:5] + t[5:6] + t[6:7]
            real = t[7:8]
            at = iota((CELLS, 128), 0) - cid
            w = (
                jnp.where(at == 0.0, (1.0 - a) * (1.0 - b) * real, 0.0)
                + jnp.where(at == 16.0, a * (1.0 - b) * real, 0.0)
                + jnp.where(at == 1.0, (1.0 - a) * b * real, 0.0)
                + jnp.where(at == 17.0, a * b * real, 0.0)
            )
            hi, lo = split2(w)
            col = pl.multiple_of(p * 128, 128)
            W_hi[:, pl.ds(col, 128)] = hi
            W_lo[:, pl.ds(col, 128)] = lo
            v = lat_state[...]
            rows_out[pl.ds(col, 128), :] = (tn(hi, v) + tn(lo, v)).astype(BF16)
            for j in (2 * p, 2 * p + 1):
                @pl.when(j != BACK)
                def _():
                    row_copy(j, cap_j).start()

            return carry

        return body

    lax.fori_loop(0, NEAR_PAIRS, make_rows(CAP_NEAR), 0)
    lax.fori_loop(NEAR_PAIRS, PAIRS, make_rows(CAP_FAR), 0)
    own_rows = slice(BACK * SLOT, BACK * SLOT + SLOT)
    rows_in[own_rows, :] = rows_out[own_rows, :]

    for n in range(8):
        ter_copy(n).wait_recv()
    lane = iota((8, 128), 1)
    quarter = jnp.floor(lane * (1.0 / 16.0))
    corner = t_in[4]
    for k in range(1, 4):
        corner = jnp.where(quarter == float(k), t_in[4 + k], corner)
    t_ext = jnp.concatenate(
        [
            jnp.broadcast_to(ter, (8, CELLS)),
            jnp.where(lane_low, t_in[0], t_in[1]),
            jnp.where(lane_low, t_in[2], t_in[3]),
            corner,
        ],
        axis=1,
    )
    lat0 = (la * 16).astype(F32)
    yr = yrow_ref[...] + lat0
    kap = jnp.zeros((8, EXT), F32)
    for k in range(8):
        kap = kap + jnp.where(t_ext == float(k), ktab[k], 0.0)
    kap = jnp.where((yr >= 0.0) & (yr < 64.0), kap, 0.0)[0:1]
    for q in range(EXT // 128):
        block = slice(128 * q, 128 * q + 128)
        eye = iota((128, EXT), 0) + float(128 * q) == iota((128, EXT), 1)
        m = adj_ref[block, :].astype(F32) * kap + jnp.where(eye, 1.0 - 4.0 * kap, 0.0)
        yc = ycol_ref[block, 0:1].astype(F32) + lat0
        m = jnp.where((yc >= 0.0) & (yc < 64.0), m, 0.0)
        Mh[block, :], Ml[block, :] = split2(m)

    def prod(ah, al, bh, bl):
        return nn(ah, bh) + (nn(ah, bl) + nn(al, bh))

    for q in range(EXT // 128):
        block = slice(128 * q, 128 * q + 128)
        m2 = prod(Mh[block, :], Ml[block, :], Mh[...], Ml[...])
        M2h[block, :], M2l[block, :] = split2(m2)
    for q in range(EXT // 128):
        block = slice(128 * q, 128 * q + 128)
        v = prod(M2h[block, :], M2l[block, :], M2h[:, 0:CELLS], M2l[:, 0:CELLS])
        Ah[block, :], Al[block, :] = split2(v)
    for q in range(CELLS // 128):
        block = slice(128 * q, 128 * q + 128)
        v = prod(M2h[block, :], M2l[block, :], M2h[...], M2l[...])
        Bh[block, :], Bl[block, :] = split2(v)

    def both_caps(body):
        def near(j, carry):
            @pl.when(j != BACK)
            def _():
                body(j, CAP_NEAR)

            return carry

        def far(j, carry):
            body(j, CAP_FAR)
            return carry

        lax.fori_loop(0, 2 * NEAR_PAIRS, near, 0)
        lax.fori_loop(2 * NEAR_PAIRS, NL, far, 0)

    both_caps(lambda j, c: row_copy(j, c).wait_recv())
    ext_f[0:CELLS, :] = tn(G[...], rows_in[...]).astype(BF16)

    def halo_copy(ext, stage, ssem, rsem, n):
        dx, dy = NEIGH[n]
        start = (256, 320, 384, 448, 512, 528, 544, 560)[n]
        size = 64 if n < 4 else 16
        if n == 0:
            src = ext.at[192:256, :]
        elif n == 1:
            src = ext.at[0:64, :]
        else:
            src = stage.at[start - 384 : start - 384 + size, :]
        return send(
            src, ext.at[start : start + size, :], ssem.at[n], rsem.at[n], lon_at(-dx), lat_at(-dy)
        )

    def halo_start(ext, stage, ssem, rsem):
        for n in range(2):
            halo_copy(ext, stage, ssem, rsem, n).start()
        stage[...] = nn(sel_ref[128:320, :], ext[0:CELLS, :]).astype(BF16)
        for n in range(2, 8):
            halo_copy(ext, stage, ssem, rsem, n).start()

    halo_start(ext_f, stage_f, s_hf, r_hf)
    for n in range(8):
        halo_copy(ext_f, stage_f, s_hf, r_hf, n).wait_recv()
    field = tn(Ah[...], ext_f[...]) + tn(Al[...], ext_f[...])

    gain = gain_ref[...]
    r = lax.rsqrt(jnp.mean(field * field, axis=1, keepdims=True) + 1e-06)
    normed = field * r
    z = (normed * gain).astype(BF16)
    z_ref[...] = z
    cot = cot_ref[...]
    react = jnp.zeros((CELLS, CH), F32)
    gz = jnp.zeros((CELLS, CH), F32)
    for h in range(4):
        part = slice(256 * h, 256 * h + 256)
        p = nn(z, w_in[:, part])
        sig = 1.0 / (1.0 + jnp.exp(-p))
        act = (p * sig).astype(BF16)
        act_ref[:, part] = act
        react = react + nn(act, w_out[part, :])
        ga = nt(cot, w_out[part, :])
        gp = (ga * sig * (1.0 + p * (1.0 - sig))).astype(BF16)
        gp_ref[:, part] = gp
        gz = gz + nt(gp, w_in[:, part])
    out_ref[...] = (field + react).astype(BF16)
    ggain = jnp.sum(gz * normed, axis=0, keepdims=True)
    gn = gz * gain
    gfield = cot.astype(F32) + r * (gn - normed * jnp.mean(gn * normed, axis=1, keepdims=True))
    g_hi, g_lo = split2(gfield)
    ext_b[0:CELLS, :] = g_hi
    halo_start(ext_b, stage_b, s_hb, r_hb)

    for h in range(2):
        half = slice(512 * h, 512 * h + 512)
        gbuf[h, 0] = tn(z_ref[...], gp_ref[:, half]).astype(BF16)
        gbuf[h, 1] = tn(act_ref[:, half], cot_ref[...]).astype(BF16)
    sib_copy = send(gbuf.at[1 - core], sib_in, s_sib, r_sib, me, sib)
    sib_copy.start()
    v_out[...] = rows_of(
        [ggain[:, 128 * k : 128 * k + 128] for k in range(4)] + [jnp.broadcast_to(over, (1, 128))],
        8, 128,
    )

    def vl_copy(d):
        return send(v_out, v_lat.at[la], s_vl.at[d], r_vl.at[d], me, lat_at(d))

    for d in range(1, NT):
        vl_copy(d).start()
    v_lat[pl.ds(la, 1)] = v_out[...].reshape(1, 8, 128)

    for n in range(8):
        halo_copy(ext_b, stage_b, s_hb, r_hb, n).wait_recv()
    gdrift = (
        nn(Bh[...], ext_b[...]) + nn(Bl[...], ext_b[...]) + nn(Bh[:, 0:CELLS], g_lo)
    ).astype(BF16)

    def gro_copy(j, cap_j):
        at = pl.multiple_of(j * SLOT, SLOT)
        return send(
            gro.at[pl.ds(at, cap_j), :], gin.at[pl.ds(at, cap_j), :],
            s_gro.at[j], r_gro.at[j], lon_at(j - BACK), la,
        )

    def bucket(cap_j):
        def body(p, carry):
            row = pl.multiple_of(p * 128, 128)
            gro[pl.ds(row, 128), :] = nn(G[pl.ds(row, 128), :], gd_ref[...]).astype(BF16)
            for j in (2 * p, 2 * p + 1):
                @pl.when(j != BACK)
                def _():
                    gro_copy(j, cap_j).start()

            return carry

        return body

    gd_ref[...] = gdrift
    lax.fori_loop(0, NEAR_PAIRS, bucket(CAP_NEAR), 0)
    lax.fori_loop(NEAR_PAIRS, PAIRS, bucket(CAP_FAR), 0)
    gin[own_rows, :] = gro[own_rows, :]

    sib_copy.wait_recv()
    for k in range(2):
        hsum[k] = (gbuf[core, k].astype(F32) + sib_in[k].astype(F32)).astype(BF16)

    def rs_copy(d):
        to = lon_at(d)
        return send(
            hsum.at[:, pl.ds(pl.multiple_of(to * 16, 16), 16), :], rs_in.at[d],
            s_rs.at[d], r_rs.at[d], to, la,
        )

    def each_other(body):
        def step(d, carry):
            body(d)
            return carry

        lax.fori_loop(1, NL, step, 0)

    each_other(lambda d: rs_copy(d).start())
    mine = pl.ds(pl.multiple_of(me * 16, 16), 16)
    rs_in[0] = hsum[:, mine, :]

    for d in range(1, NT):
        vl_copy(d).wait_recv()
    v_sum[...] = v_lat[0] + v_lat[1] + v_lat[2] + v_lat[3]

    def vn_copy(d):
        return send(v_sum, v_lon.at[me], s_vn.at[d], r_vn.at[d], lon_at(d), la)

    each_other(lambda d: vn_copy(d).start())
    v_lon[pl.ds(me, 1)] = v_sum[...].reshape(1, 8, 128)

    both_caps(lambda j, c: gro_copy(j, c).wait_recv())
    grad_ref[...] = (nn(W_hi[...], gin[...]) + nn(W_lo[...], gin[...])).astype(BF16)

    each_other(lambda d: rs_copy(d).wait_recv())
    acc = jnp.zeros((2, 16, CH), F32)
    for d in range(NL):
        acc = acc + rs_in[d].astype(F32)
    xh_out[...] = acc
    xh_copy = send(xh_out, xh_in, s_xh, r_xh, me, opp)
    xh_copy.start()
    xh_copy.wait_recv()
    gout[core, :, mine, :] = (xh_out[...] + xh_in[...]).astype(BF16)

    def ag_copy(d):
        piece = gout.at[core, :, mine, :]
        return send(piece, piece, s_ag.at[d], r_ag.at[d], lon_at(d), la)

    each_other(lambda d: ag_copy(d).start())
    each_other(lambda d: vn_copy(d).wait_recv())
    total = v_lon[0]
    for k in range(1, NL):
        total = total + v_lon[k]
    vec_ref[...] = total
    each_other(lambda d: ag_copy(d).wait_recv())
    fin = send(gout.at[core], gout.at[core], s_fin, r_fin, me, sib)
    fin.start()

    each_pair(lambda j: req_copy(j).wait_send())
    for n in range(8):
        ter_copy(n).wait_send()
        halo_copy(ext_f, stage_f, s_hf, r_hf, n).wait_send()
        halo_copy(ext_b, stage_b, s_hb, r_hb, n).wait_send()
    both_caps(lambda j, c: row_copy(j, c).wait_send())
    both_caps(lambda j, c: gro_copy(j, c).wait_send())
    sib_copy.wait_send()
    for d in range(1, NT):
        vl_copy(d).wait_send()
    each_other(lambda d: rs_copy(d).wait_send())
    each_other(lambda d: vn_copy(d).wait_send())
    xh_copy.wait_send()
    each_other(lambda d: ag_copy(d).wait_send())
    fin.wait()


def step_kernel(state, cot, w_in, w_out, gain, sb, cc, fa, fb, ter, ktab):
    adj, ycol, yrow, sel, spread = tables()
    vm = lambda *s, t=BF16: pltpu.VMEM(s, t)
    dma = lambda *s: pltpu.SemaphoreType.DMA(s)
    one = pltpu.SemaphoreType.DMA
    scratch = [
        vm(NS, CELLS), vm(CELLS, NS), vm(CELLS, NS), vm(NS, CH), vm(NS, CH), vm(NS, CH), vm(NS, CH),
        vm(PAIRS, 8, 128, t=F32), vm(NL, 8, 128, t=F32), vm(3, 8, 128, t=F32), vm(8, 8, 128, t=F32),
        vm(EXT, CH), vm(EXT, CH), vm(192, CH), vm(192, CH), vm(CELLS, CH),
        vm(EXT, EXT), vm(EXT, EXT), vm(EXT, EXT), vm(EXT, EXT),
        vm(EXT, CELLS), vm(EXT, CELLS), vm(CELLS, EXT), vm(CELLS, EXT),
        vm(CELLS, CH), vm(CELLS, HID), vm(CELLS, HID),
        vm(2, 2, 512, 512), vm(2, 512, 512), vm(2, 512, 512), vm(NL, 2, 16, 512),
        vm(2, 16, 512, t=F32), vm(2, 16, 512, t=F32),
        vm(8, 128, t=F32), vm(NT, 8, 128, t=F32), vm(8, 128, t=F32), vm(NL, 8, 128, t=F32),
        dma(NL), dma(NL), dma(NL), dma(NL), dma(NL), dma(NL), dma(8), dma(8), dma(8), dma(8),
        dma(8), dma(8), one, one, dma(NL), dma(NL), one, one, dma(NL), dma(NL), one, one,
        dma(NT), dma(NT), dma(NL), dma(NL),
    ]
    vmem = pl.BlockSpec(memory_space=pltpu.VMEM)
    smem = pl.BlockSpec(memory_space=pltpu.SMEM)
    return pl.pallas_call(
        kernel,
        out_shape=(
            jax.ShapeDtypeStruct((CELLS, CH), BF16),
            jax.ShapeDtypeStruct((CELLS, CH), BF16),
            jax.ShapeDtypeStruct((2, 2, 512, 512), BF16),
            jax.ShapeDtypeStruct((8, 128), F32),
        ),
        in_specs=[vmem] * 10 + [smem] + [vmem] * 5,
        out_specs=(vmem,) * 4,
        scratch_shapes=scratch,
        compiler_params=pltpu.CompilerParams(
            collective_id=0, has_side_effects=True, vmem_limit_bytes=60 * 1024 * 1024
        ),
        cost_estimate=pl.CostEstimate(
            flops=12 * 10**9, bytes_accessed=8 * 2**20, transcendentals=CELLS * HID
        ),
    )(
        state, cot, w_in, w_out, gain.reshape(1, CH), sb, cc, fa, fb, ter, ktab,
        jnp.asarray(adj, BF16), jnp.asarray(ycol, BF16), jnp.asarray(yrow, F32),
        jnp.asarray(sel, BF16), jnp.asarray(spread, F32),
    )


def on_device(*args):
    state, cot = (v.reshape(CELLS, CH) for v in args[:2])
    state_out, state_grad, grads, vec = step_kernel(state, cot, *args[2:])
    over = vec[4, 0]

    def fast(state_out, state_grad, grads, vec, *rest):
        inner = grads[:, 0].transpose(1, 0, 2).reshape(CH, HID).astype(F32)
        outer = grads[:, 1].reshape(HID, CH).astype(F32)
        shape = (16, 16, CH)
        return state_out.reshape(shape), state_grad.reshape(shape), inner, outer, vec[0:4].reshape(CH)

    def general(state_out, state_grad, grads, vec, *rest):
        return on_device_general(*rest)

    return lax.cond(over > 0.0, general, fast, state_out, state_grad, grads, vec, *args)


def solution(mesh):
    placed = (
        P("lon", "lat", None),
        P("lon", "lat", None),
        P(),
        P(),
        P(),
        P("lon", "lat"),
        P("lon", "lat"),
        P("lon", "lat"),
        P("lon", "lat"),
        P("lon", "lat"),
        P(),
    )
    return jax.shard_map(
        on_device,
        mesh=mesh,
        in_specs=placed,
        out_specs=(P("lon", "lat", None), P("lon", "lat", None), P(), P(), P()),
        check_vma=False,
    )
```

```python
import functools

import jax
import jax.numpy as jnp
import numpy as np
from jax import lax
from jax.experimental import pallas as pl
from jax.experimental.pallas import tpu as pltpu
from jax.sharding import PartitionSpec as P

MESH = pl.DeviceIdType.MESH
F32 = jnp.float32
BF16 = jnp.bfloat16
NL = 32
NT = 4
CELLS = 256
CH = 512
HID = 1024
SLOT = 64
NS = NL * SLOT
PAIRS = NL // 2
NEAR_PAIRS = 7
CAPS = ((32, 32), (48, 16))
BACK = 6
EXT = 640
NEIGH = ((-1, 0), (1, 0), (0, -1), (0, 1), (-1, -1), (-1, 1), (1, -1), (1, 1))


def ext_cells():
    cells = [(x, y) for x in range(16) for y in range(16)]
    low, mid, top = range(-4, 0), range(16), range(16, 20)
    for dx, dy in NEIGH:
        xs = (low, mid, top)[dx + 1]
        ys = (low, mid, top)[dy + 1]
        cells += [(x, y) for x in xs for y in ys]
    return np.array(cells)


def tables():
    cells = ext_cells()
    count = len(cells)
    dist = np.abs(cells[:, None] - cells[None, :]).sum(-1)
    adj = np.zeros((EXT, EXT), np.float32)
    adj[:count, :count] = dist == 1
    ys = np.full((EXT,), -1000.0, np.float32)
    ys[:count] = cells[:, 1]
    ycol = np.broadcast_to(ys[:, None], (EXT, 128))
    yrow = ys[None, :]
    sel = np.zeros((384, CELLS), np.float32)
    at = 0
    for dx, dy in NEIGH:
        width = (4 if dx else 16) * (4 if dy else 16)
        for q in range(width):
            x, y = cells[256 + at + q]
            sel[at + q, (x - 16 * dx) * 16 + (y - 16 * dy)] = 1.0
        at += width
    spread = (np.arange(256)[None, :] % 16 == np.arange(16)[:, None]).astype(np.float32)
    return adj, ycol, yrow, sel, spread


def nn(a, b):
    return jnp.dot(a, b, preferred_element_type=F32)


def nt(a, b):
    return lax.dot_general(a, b, (((1,), (1,)), ((), ())), preferred_element_type=F32)


def tn(a, b):
    return lax.dot_general(a, b, (((0,), (0,)), ((), ())), preferred_element_type=F32)


def split2(v):
    hi = v.astype(BF16)
    return hi, (v - hi.astype(F32)).astype(BF16)


def iota(shape, dim):
    return lax.broadcasted_iota(jnp.int32, shape, dim).astype(F32)

STEPS = 4


def ring_pass(value, axis):
    size = lax.axis_size(axis)
    return lax.ppermute(value, axis, [(i, (i + 1) % size) for i in range(size)])


def ring_gather(value):
    size, me = lax.axis_size("lon"), lax.axis_index("lon")
    rows = value.shape[0]

    def step(k, carry):
        block, out = carry
        out = lax.dynamic_update_slice_in_dim(out, block, (me - k) % size * rows, 0)
        return ring_pass(block, "lon"), out

    out = jnp.zeros((size * rows,) + value.shape[1:], value.dtype)
    return lax.fori_loop(0, size, step, (value, out))[1]


def ring_scatter(value, rows):
    size, me = lax.axis_size("lon"), lax.axis_index("lon")

    def own(k):
        return lax.dynamic_slice_in_dim(value, (me + size - 1 - k) % size * rows, rows, 0)

    total = lax.fori_loop(1, size, lambda k, acc: ring_pass(acc, "lon") + own(k), own(0))
    return total.astype(jnp.bfloat16)


def ring_total(value):
    for repeat in range(2):
        for axis in ("lon", "lat"):
            def step(k, carry):
                block, total = carry
                block = ring_pass(block, axis)
                return block, total + block

            value = lax.fori_loop(1, lax.axis_size(axis), step, (value, value))[1]
        if repeat == 0:
            first = jnp.logical_and(lax.axis_index("lon") == 0, lax.axis_index("lat") == 0)
            value = jnp.where(first, value, 0.0)
    return value


def with_halo(value, sides, width, wrap):
    for axis, dim in sides:
        size, length = (lax.axis_size(axis), value.shape[dim])
        up = [(i, (i + 1) % size) for i in range(size if wrap else size - 1)]
        down = [(j, i) for i, j in up]
        last = lax.slice_in_dim(value, length - width, length, axis=dim)
        first = lax.slice_in_dim(value, 0, width, axis=dim)
        before = lax.ppermute(last, axis, up)
        after = lax.ppermute(first, axis, down)
        value = jnp.concatenate([before, value, after], axis=dim)
    return value


def flat_sources(source_block, corner_code, lat_cells):
    per_row = lat_cells // 8
    lon_part = source_block // per_row * 8 + corner_code // 8
    lat_part = source_block % per_row * 8 + corner_code % 8
    return lon_part * lat_cells + lat_part


def corner_table(flat_ids, frac_a, frac_b, lat_cells):
    shifted = jnp.stack([flat_ids, flat_ids + lat_cells, flat_ids + 1, flat_ids + lat_cells + 1])
    weights = jnp.stack(
        [
            (1.0 - frac_a) * (1.0 - frac_b),
            frac_a * (1.0 - frac_b),
            (1.0 - frac_a) * frac_b,
            frac_a * frac_b,
        ]
    )
    return (shifted, weights)


def laplace(field):
    wide = with_halo(field.astype(jnp.bfloat16), (("lon", 0),), 1, True).astype(field.dtype)
    tall = with_halo(field.astype(jnp.bfloat16), (("lat", 1),), 1, False).astype(field.dtype)
    return wide[2:] + wide[:-2] + tall[:, 2:] + tall[:, :-2] - 4.0 * field


def on_device_general(
    latent_state,
    cotangent,
    w_inner,
    w_outer,
    norm_gain,
    source_block,
    corner_code,
    frac_lon,
    frac_lat,
    terrain,
    kappa_table,
):
    lon_cells, lat_cells, chans = latent_state.shape
    cells = lon_cells * lat_cells
    flat_ids = flat_sources(source_block, corner_code, lat_cells)
    shifted, weights = corner_table(
        flat_ids.reshape(cells), frac_lon.reshape(cells), frac_lat.reshape(cells), lat_cells
    )
    shard_piece = ring_gather(latent_state)
    count = shard_piece.shape[0] * lat_cells
    local = shifted
    hits = local[:, :, None] == jnp.arange(count, dtype=jnp.int32)[None, None, :]
    select = jnp.sum(jnp.where(hits, weights[:, :, None], 0.0), 0)
    upper = select.astype(jnp.bfloat16)
    lower = (select - upper.astype(jnp.float32)).astype(jnp.bfloat16)
    values = shard_piece.reshape(count, chans)
    running = jnp.dot(upper, values, preferred_element_type=jnp.float32)
    drift = running + jnp.dot(lower, values, preferred_element_type=jnp.float32)
    drift = drift.reshape(lon_cells, lat_cells, chans)
    classes = jnp.arange(kappa_table.shape[0], dtype=jnp.int32)
    kappa = jnp.sum(jnp.where(terrain[..., None] == classes, kappa_table, 0.0), -1)[..., None]
    field = drift
    for turn_index in range(STEPS):
        field = field + kappa * laplace(field)
    flat_field = field.reshape(cells, chans)
    rstd = lax.rsqrt(jnp.mean(flat_field * flat_field, -1, keepdims=True) + 1e-06)
    normed = flat_field * rstd
    z_in = (normed * norm_gain).astype(jnp.bfloat16)
    pre_act = jnp.dot(z_in, w_inner, preferred_element_type=jnp.float32)
    act = jax.nn.silu(pre_act).astype(jnp.bfloat16)
    react = jnp.dot(act, w_outer, preferred_element_type=jnp.float32)
    state_out = (flat_field + react).astype(jnp.bfloat16).reshape(lon_cells, lat_cells, chans)
    cot = cotangent.reshape(cells, chans)
    local_outer = jnp.dot(act.T, cot, preferred_element_type=jnp.float32)
    grad_act = jnp.dot(cot, w_outer.T, preferred_element_type=jnp.float32)
    sigma = jax.nn.sigmoid(pre_act)
    grad_pre = (grad_act * sigma * (1.0 + pre_act * (1.0 - sigma))).astype(jnp.bfloat16)
    local_inner = jnp.dot(z_in.T, grad_pre, preferred_element_type=jnp.float32)
    grad_z = jnp.dot(grad_pre, w_inner.T, preferred_element_type=jnp.float32)
    local_gain = jnp.sum(grad_z * normed, 0)
    grad_norm = grad_z * norm_gain
    grad_field = cot.astype(jnp.float32) + rstd * (
        grad_norm - normed * jnp.mean(grad_norm * normed, -1, keepdims=True)
    )
    grad_field = grad_field.reshape(lon_cells, lat_cells, chans)
    for turn_index in range(STEPS):
        grad_field = grad_field + laplace(kappa * grad_field)
    grad_drift = grad_field.astype(jnp.bfloat16)
    parts = (weights[:, :, None] * grad_drift.reshape(cells, chans).astype(jnp.float32)).astype(
        jnp.bfloat16
    )
    count = lon_cells * lax.axis_size("lon")
    width = count * lat_cells
    local = shifted
    onehot = (local[:, :, None] == jnp.arange(width, dtype=jnp.int32)[None, None, :]).astype(
        jnp.bfloat16
    )
    term = jnp.einsum("ksr,ksc->rc", onehot, parts, preferred_element_type=jnp.float32)
    summed = ring_scatter(term.reshape(count, lat_cells, chans), lon_cells)
    grad_inner, grad_outer, grad_gain = (
        ring_total(v) for v in (local_inner, local_outer, local_gain)
    )
    return (state_out, summed, grad_inner, grad_outer, grad_gain)


def kernel(
    lat_state, cot_ref, w_in, w_out, gain_ref, sb_ref, cc_ref, fa_ref, fb_ref, ter_ref, ktab,
    adj_ref, ycol_ref, yrow_ref, sel_ref, spread_ref,
    out_ref, grad_ref, gi_ref, go_ref, gg_ref, over_ref,
    gout, G, W_hi, W_lo, rows_out, rows_in, gro, gin, req_out, req_in, t_out, t_in,
    ext_f, ext_b, stage_f, stage_b, gd_ref, acc_ref, Mh, Ml, M2h, M2l, Ah, Al, Bh, Bl,
    z_ref, p_ref, gp_ref, gbuf, sib_in, hsum, rs_in, xh_out, xh_in, v_out, v_lat, v_sum, v_lon,
    s_req, r_req, s_row, r_row, s_gro, r_gro, s_ter, r_ter, s_hf, r_hf, s_hb, r_hb,
    s_sib, r_sib, s_rs, r_rs, s_xh, r_xh, s_ag, r_ag, s_fin, r_fin, s_vl, r_vl, s_vn, r_vn,
):
    me = lax.axis_index("lon")
    la = lax.axis_index("lat")
    core = lax.rem(la, 2)
    sib = la + 1 - 2 * core
    opp = lax.rem(la + 2, NT)

    inside = jnp.logical_and(la > 0, la < NT - 1)

    def sized(far, body):
        for kind, flag in ((0, jnp.logical_not(inside)), (1, inside)):
            @pl.when(flag)
            def _():
                body(CAPS[kind][far])

    def lon_at(d):
        return lax.rem(me + d + 2 * NL, NL)

    def lat_at(d):
        return lax.rem(la + d + NT, NT)

    def send(src, dst, ssem, rsem, lon, lat):
        return pltpu.make_async_remote_copy(
            src_ref=src, dst_ref=dst, send_sem=ssem, recv_sem=rsem,
            device_id=(lon, lat), device_id_type=MESH,
        )

    rows_in[...] = jnp.zeros((NS, CH), BF16)
    gin[...] = jnp.zeros((NS, CH), BF16)
    ext_f[576:EXT, :] = jnp.zeros((EXT - 576, CH), BF16)
    ext_b[576:EXT, :] = jnp.zeros((EXT - 576, CH), BF16)

    barrier = pltpu.get_barrier_semaphore()

    def greet(d, carry):
        pl.semaphore_signal(barrier, inc=1, device_id=(lon_at(d), la), device_id_type=MESH)
        return carry

    lax.fori_loop(1, NL, greet, 0)
    for dx, dy in NEIGH[2:]:
        pl.semaphore_signal(
            barrier, inc=1, device_id=(lon_at(dx), lat_at(dy)), device_id_type=MESH
        )
    pl.semaphore_signal(barrier, inc=1, device_id=(me, opp), device_id_type=MESH)

    raw = jnp.concatenate(
        [
            sb_ref[...].astype(F32), cc_ref[...].astype(F32), fa_ref[...], fb_ref[...],
            ter_ref[...].astype(F32),
        ],
        axis=0,
    )
    flat = jnp.dot(
        raw, spread_ref[...], precision=lax.Precision.HIGHEST, preferred_element_type=F32
    )
    own = jnp.floor(iota((16, CELLS), 1) * (1.0 / 16.0)) == iota((16, CELLS), 0)

    def line(k):
        return jnp.sum(jnp.where(own, flat[16 * k : 16 * k + 16], 0.0), 0, keepdims=True)

    sb, cc, fa, fb, ter = (line(k) for k in range(5))
    dev = jnp.floor(sb * 0.25)
    blon = jnp.floor(sb * 0.5)
    klon = jnp.floor(cc * 0.125)
    cell = ((blon - 2.0 * dev) * 8.0 + klon) * 16.0 + (sb - 2.0 * blon) * 8.0 + (cc - 8.0 * klon)
    slot = dev - me.astype(F32) + float(BACK)
    slot = jnp.where(slot < 0.0, slot + float(NL), slot)
    slot = jnp.where(slot >= float(NL), slot - float(NL), slot)
    hits = iota((NL, CELLS), 0) == slot
    before = (iota((CELLS, CELLS), 0) < iota((CELLS, CELLS), 1)).astype(F32).astype(BF16)
    counts = nn(jnp.where(hits, 1.0, 0.0).astype(BF16), before)
    rank = jnp.sum(jnp.where(hits, counts, 0.0), 0, keepdims=True)
    near_cap = jnp.where(inside, float(CAPS[1][0]), float(CAPS[0][0]))
    far_cap = jnp.where(inside, float(CAPS[1][1]), float(CAPS[0][1]))
    cap = jnp.where(slot < 2.0 * NEAR_PAIRS, near_cap, far_cap)
    fits = rank < cap
    place = jnp.where(fits, slot * float(SLOT) + rank, -1.0)
    over = jnp.sum(jnp.where(fits, 0.0, 1.0), axis=1, keepdims=True)

    def fill_g(q, carry):
        row = pl.multiple_of(q * 128, 128)
        at = iota((128, CELLS), 0) + lax.convert_element_type(row, F32)
        G[pl.ds(row, 128), :] = jnp.where(at == place, 1.0, 0.0).astype(BF16)
        return carry

    lax.fori_loop(0, PAIRS, fill_g, 0)

    def rows_of(lines, height, width):
        which = iota((height, width), 0)
        out = jnp.zeros((height, width), F32)
        for k, v in enumerate(lines):
            out = out + jnp.where(which == float(k), v, 0.0)
        return out

    fah = fa.astype(BF16).astype(F32)
    fam = (fa - fah).astype(BF16).astype(F32)
    fbh = fb.astype(BF16).astype(F32)
    fbm = (fb - fbh).astype(BF16).astype(F32)
    params = rows_of(
        [cell, fah, fam, fa - fah - fam, fbh, fbm, fb - fbh - fbm, jnp.ones_like(fa)], 16, CELLS
    ).astype(BF16)

    def fill_req(p, carry):
        req_out[p] = nt(params, G[pl.ds(pl.multiple_of(p * 128, 128), 128), :])[0:8]
        return carry

    lax.fori_loop(0, PAIRS, fill_req, 0)
    t_all = nt(jnp.broadcast_to(ter, (16, CELLS)).astype(BF16), sel_ref[...])
    for q in range(3):
        t_out[q] = t_all[0:8, 128 * q : 128 * q + 128]

    pl.semaphore_wait(barrier, NL - 1 + 7)

    def req_copy(j):
        return send(
            req_out.at[j // 2], req_in.at[j], s_req.at[j], r_req.at[j], lon_at(j - BACK), la
        )

    def each_pair(body):
        def step(j, carry):
            @pl.when(j != BACK)
            def _():
                body(j)

            return carry

        lax.fori_loop(0, NL, step, 0)

    each_pair(lambda j: req_copy(j).start())

    def ter_copy(n):
        dx, dy = NEIGH[n]
        tile = (0, 0, 1, 1, 2, 2, 2, 2)[n]
        return send(
            t_out.at[tile], t_in.at[n], s_ter.at[n], r_ter.at[n], lon_at(-dx), lat_at(-dy)
        )

    for n in range(8):
        ter_copy(n).start()
    req_in[BACK] = req_out[BACK // 2]

    each_pair(lambda j: req_copy(j).wait_recv())
    lane_low = iota((8, 128), 1) < float(SLOT)

    def row_copy(j, cap_j):
        at = pl.multiple_of(j * SLOT, SLOT)
        return send(
            rows_out.at[pl.ds(at, cap_j), :], rows_in.at[pl.ds(at, cap_j), :],
            s_row.at[j], r_row.at[j], lon_at(BACK - j), la,
        )

    def make_rows(far):
        def body(p, carry):
            t = jnp.where(lane_low, req_in[2 * p], req_in[2 * p + 1])
            cid = t[0:1]
            a = t[1:2] + t[2:3] + t[3:4]
            b = t[4:5] + t[5:6] + t[6:7]
            real = t[7:8]
            at = iota((CELLS, 128), 0) - cid
            w = (
                jnp.where(at == 0.0, (1.0 - a) * (1.0 - b) * real, 0.0)
                + jnp.where(at == 16.0, a * (1.0 - b) * real, 0.0)
                + jnp.where(at == 1.0, (1.0 - a) * b * real, 0.0)
                + jnp.where(at == 17.0, a * b * real, 0.0)
            )
            hi, lo = split2(w)
            col = pl.multiple_of(p * 128, 128)
            W_hi[:, pl.ds(col, 128)] = hi
            W_lo[:, pl.ds(col, 128)] = lo
            v = lat_state[...]
            rows_out[pl.ds(col, 128), :] = (tn(hi, v) + tn(lo, v)).astype(BF16)
            for j in (2 * p, 2 * p + 1):
                @pl.when(j != BACK)
                def _():
                    sized(far, lambda c: row_copy(j, c).start())

            return carry

        return body

    lax.fori_loop(0, NEAR_PAIRS, make_rows(0), 0)
    lax.fori_loop(NEAR_PAIRS, PAIRS, make_rows(1), 0)
    own_rows = slice(BACK * SLOT, BACK * SLOT + SLOT)
    rows_in[own_rows, :] = rows_out[own_rows, :]

    for n in range(8):
        ter_copy(n).wait_recv()
    lane = iota((8, 128), 1)
    quarter = jnp.floor(lane * (1.0 / 16.0))
    corner = t_in[4]
    for k in range(1, 4):
        corner = jnp.where(quarter == float(k), t_in[4 + k], corner)
    t_ext = jnp.concatenate(
        [
            jnp.broadcast_to(ter, (8, CELLS)),
            jnp.where(lane_low, t_in[0], t_in[1]),
            jnp.where(lane_low, t_in[2], t_in[3]),
            corner,
        ],
        axis=1,
    )
    lat0 = (la * 16).astype(F32)
    yr = yrow_ref[...] + lat0
    kap = jnp.zeros((8, EXT), F32)
    for k in range(8):
        kap = kap + jnp.where(t_ext == float(k), ktab[k], 0.0)
    kap = jnp.where((yr >= 0.0) & (yr < 64.0), kap[0:1], 0.0)
    def blocks(count, body):
        def step(q, carry):
            body(pl.ds(pl.multiple_of(q * 128, 128), 128), q * 128)
            return carry

        lax.fori_loop(0, count, step, 0)

    def fill_m(block, row):
        eye = iota((128, EXT), 0) + lax.convert_element_type(row, F32) == iota((128, EXT), 1)
        m = adj_ref[block, :].astype(F32) * kap + jnp.where(eye, 1.0 - 4.0 * kap, 0.0)
        yc = ycol_ref[block, 0:1].astype(F32) + lat0
        m = jnp.where((yc >= 0.0) & (yc < 64.0), m, 0.0)
        Mh[block, :], Ml[block, :] = split2(m)

    blocks(EXT // 128, fill_m)

    def prod(ah, al, bh, bl):
        return nn(ah, bh) + (nn(ah, bl) + nn(al, bh))

    def square(block, row):
        m2 = prod(Mh[block, :], Ml[block, :], Mh[...], Ml[...])
        M2h[block, :], M2l[block, :] = split2(m2)

    def last_a(block, row):
        v = prod(M2h[block, :], M2l[block, :], M2h[:, 0:CELLS], M2l[:, 0:CELLS])
        Ah[block, :], Al[block, :] = split2(v)

    def last_b(block, row):
        v = prod(M2h[block, :], M2l[block, :], M2h[...], M2l[...])
        Bh[block, :], Bl[block, :] = split2(v)

    blocks(EXT // 128, square)
    blocks(EXT // 128, last_a)
    blocks(CELLS // 128, last_b)

    def both_caps(body):
        def near(j, carry):
            @pl.when(j != BACK)
            def _():
                sized(0, lambda c: body(j, c))

            return carry

        def far(j, carry):
            sized(1, lambda c: body(j, c))
            return carry

        lax.fori_loop(0, 2 * NEAR_PAIRS, near, 0)
        lax.fori_loop(2 * NEAR_PAIRS, NL, far, 0)

    both_caps(lambda j, c: row_copy(j, c).wait_recv())

    def put_rows(k, acc):
        part = pl.ds(pl.multiple_of(k * 512, 512), 512)
        acc_ref[...] += tn(G[part, :], rows_in[part, :])
        return acc

    acc_ref[...] = jnp.zeros((CELLS, CH), F32)
    lax.fori_loop(0, NS // 512, put_rows, 0)
    ext_f[0:CELLS, :] = acc_ref[...].astype(BF16)

    def halo_copy(ext, stage, ssem, rsem, n):
        dx, dy = NEIGH[n]
        start = (256, 320, 384, 448, 512, 528, 544, 560)[n]
        size = 64 if n < 4 else 16
        if n == 0:
            src = ext.at[192:256, :]
        elif n == 1:
            src = ext.at[0:64, :]
        else:
            src = stage.at[start - 384 : start - 384 + size, :]
        return send(
            src, ext.at[start : start + size, :], ssem.at[n], rsem.at[n], lon_at(-dx), lat_at(-dy)
        )

    def halo_start(ext, stage, ssem, rsem):
        for n in range(2):
            halo_copy(ext, stage, ssem, rsem, n).start()
        stage[...] = nn(sel_ref[128:320, :], ext[0:CELLS, :]).astype(BF16)
        for n in range(2, 8):
            halo_copy(ext, stage, ssem, rsem, n).start()

    halo_start(ext_f, stage_f, s_hf, r_hf)
    for n in range(8):
        halo_copy(ext_f, stage_f, s_hf, r_hf, n).wait_recv()
    field = tn(Ah[...], ext_f[...]) + tn(Al[...], ext_f[...])

    def sib_copy(k):
        return send(gbuf.at[1 - core, k], sib_in.at[k], s_sib.at[k], r_sib.at[k], me, sib)

    gain = gain_ref[...]
    r = lax.rsqrt(jnp.mean(field * field, axis=1, keepdims=True) + 1e-06)
    normed = field * r
    z_ref[...] = (normed * gain).astype(BF16)
    cot = cot_ref[...]
    acc_ref[...] = field

    def forward(h, carry):
        part = pl.ds(pl.multiple_of(h * 256, 256), 256)
        p = nn(z_ref[...], w_in[:, part])
        p_ref[:, part] = p
        act = (p * (1.0 / (1.0 + jnp.exp(-p)))).astype(BF16)
        gbuf[h // 2, 1, pl.ds(lax.rem(h, 2) * 256, 256), :] = tn(act, cot_ref[...]).astype(BF16)
        acc_ref[...] += nn(act, w_out[part, :])
        return carry

    lax.fori_loop(0, 4, forward, 0)
    sib_copy(1).start()
    out_ref[...] = acc_ref[...].astype(BF16)
    acc_ref[...] = jnp.zeros((CELLS, CH), F32)

    def backward(h, carry):
        part = pl.ds(pl.multiple_of(h * 256, 256), 256)
        ga = nt(cot_ref[...], w_out[part, :])
        p = p_ref[:, part]
        sig = 1.0 / (1.0 + jnp.exp(-p))
        gp = (ga * sig * (1.0 + p * (1.0 - sig))).astype(BF16)
        gp_ref[:, part] = gp
        acc_ref[...] += nt(gp, w_in[:, part])
        return carry

    lax.fori_loop(0, 4, backward, 0)
    gz = acc_ref[...]
    ggain = jnp.sum(gz * normed, axis=0, keepdims=True)
    gn = gz * gain
    gfield = cot.astype(F32) + r * (gn - normed * jnp.mean(gn * normed, axis=1, keepdims=True))
    g_hi, g_lo = split2(gfield)
    ext_b[0:CELLS, :] = g_hi
    halo_start(ext_b, stage_b, s_hb, r_hb)

    def inner_half(h, carry):
        half = pl.ds(pl.multiple_of(h * 512, 512), 512)
        gbuf[h, 0] = tn(z_ref[...], gp_ref[:, half]).astype(BF16)
        return carry

    lax.fori_loop(0, 2, inner_half, 0)
    sib_copy(0).start()
    v_out[...] = rows_of(
        [ggain[:, 128 * k : 128 * k + 128] for k in range(4)] + [jnp.broadcast_to(over, (1, 128))],
        8, 128,
    )

    def vl_copy(d):
        return send(v_out, v_lat.at[la], s_vl.at[d], r_vl.at[d], me, lat_at(d))

    for d in range(1, NT):
        vl_copy(d).start()
    v_lat[pl.ds(la, 1)] = v_out[...].reshape(1, 8, 128)

    def rs_copy(d):
        to = lon_at(d)
        return send(
            hsum.at[:, pl.ds(pl.multiple_of(to * 16, 16), 16), :], rs_in.at[d],
            s_rs.at[d], r_rs.at[d], to, la,
        )

    def each_other(body):
        def step(d, carry):
            body(d)
            return carry

        lax.fori_loop(1, NL, step, 0)

    for k in (1, 0):
        sib_copy(k).wait_recv()
        hsum[k] = (gbuf[core, k].astype(F32) + sib_in[k].astype(F32)).astype(BF16)
    each_other(lambda d: rs_copy(d).start())
    mine = pl.ds(pl.multiple_of(me * 16, 16), 16)
    rs_in[0] = hsum[:, mine, :]

    for n in range(8):
        halo_copy(ext_b, stage_b, s_hb, r_hb, n).wait_recv()
    gdrift = (
        nn(Bh[...], ext_b[...]) + nn(Bl[...], ext_b[...]) + nn(Bh[:, 0:CELLS], g_lo)
    ).astype(BF16)

    def gro_copy(j, cap_j):
        at = pl.multiple_of(j * SLOT, SLOT)
        return send(
            gro.at[pl.ds(at, cap_j), :], gin.at[pl.ds(at, cap_j), :],
            s_gro.at[j], r_gro.at[j], lon_at(j - BACK), la,
        )

    def bucket(far):
        def body(p, carry):
            row = pl.multiple_of(p * 128, 128)
            gro[pl.ds(row, 128), :] = nn(G[pl.ds(row, 128), :], gd_ref[...]).astype(BF16)
            for j in (2 * p, 2 * p + 1):
                @pl.when(j != BACK)
                def _():
                    sized(far, lambda c: gro_copy(j, c).start())

            return carry

        return body

    gd_ref[...] = gdrift
    lax.fori_loop(0, NEAR_PAIRS, bucket(0), 0)
    lax.fori_loop(NEAR_PAIRS, PAIRS, bucket(1), 0)
    gin[own_rows, :] = gro[own_rows, :]

    for d in range(1, NT):
        vl_copy(d).wait_recv()
    v_sum[...] = v_lat[0] + v_lat[1] + v_lat[2] + v_lat[3]

    def vn_copy(d):
        return send(v_sum, v_lon.at[me], s_vn.at[d], r_vn.at[d], lon_at(d), la)

    each_other(lambda d: vn_copy(d).start())
    v_lon[pl.ds(me, 1)] = v_sum[...].reshape(1, 8, 128)

    each_other(lambda d: rs_copy(d).wait_recv())
    xh_out[...] = lax.fori_loop(
        0, NL, lambda d, acc: acc + rs_in[d].astype(F32), jnp.zeros((2, 16, CH), F32)
    )
    xh_copy = send(xh_out, xh_in, s_xh, r_xh, me, opp)
    xh_copy.start()
    xh_copy.wait_recv()
    gout[core, :, mine, :] = (xh_out[...] + xh_in[...]).astype(BF16)

    def ag_copy(d):
        piece = gout.at[core, :, mine, :]
        return send(piece, piece, s_ag.at[d], r_ag.at[me], lon_at(d), la)

    def ag_wait(q):
        piece = gout.at[core, :, pl.ds(pl.multiple_of(q * 16, 16), 16), :]
        send(piece, piece, s_ag.at[q], r_ag.at[q], q, la).wait_recv()

    each_other(lambda d: ag_copy(d).start())
    both_caps(lambda j, c: gro_copy(j, c).wait_recv())

    def scatter(k, carry):
        part = pl.ds(pl.multiple_of(k * 512, 512), 512)
        acc_ref[...] += nn(W_hi[:, part], gin[part, :]) + nn(W_lo[:, part], gin[part, :])
        return carry

    acc_ref[...] = jnp.zeros((CELLS, CH), F32)
    lax.fori_loop(0, NS // 512, scatter, 0)
    grad_ref[...] = acc_ref[...].astype(BF16)

    each_other(lambda d: vn_copy(d).wait_recv())
    total = v_lon[0]
    for k in range(1, NL):
        total = total + v_lon[k]
    for k in range(4):
        gg_ref[0:1, 128 * k : 128 * k + 128] = total[k : k + 1]
    over_ref[...] = total[4:5, 0:1]

    def fin_copy(c):
        piece = gout.at[core, :, 128 * c : 128 * c + 128, :]
        return send(piece, piece, s_fin.at[c], r_fin.at[c], me, sib)

    def leave(half, c):
        rows = slice(128 * c, 128 * c + 128)
        left = pl.ds(pl.multiple_of(half * 512, 512), 512)
        below = pl.ds(pl.multiple_of(half * 512 + 128 * c, 128), 128)
        gi_ref[rows, left] = gout[half, 0, rows, :]
        go_ref[below, :] = gout[half, 1, rows, :]

    for c in range(4):
        def arrive(q, carry):
            @pl.when(q != me)
            def _():
                ag_wait(q)

            return carry

        lax.fori_loop(8 * c, 8 * c + 8, arrive, 0)
        fin_copy(c).start()
        leave(core, c)

    each_pair(lambda j: req_copy(j).wait_send())
    for n in range(8):
        ter_copy(n).wait_send()
        halo_copy(ext_f, stage_f, s_hf, r_hf, n).wait_send()
        halo_copy(ext_b, stage_b, s_hb, r_hb, n).wait_send()
    both_caps(lambda j, c: row_copy(j, c).wait_send())
    both_caps(lambda j, c: gro_copy(j, c).wait_send())
    sib_copy(0).wait_send()
    sib_copy(1).wait_send()
    for d in range(1, NT):
        vl_copy(d).wait_send()
    each_other(lambda d: rs_copy(d).wait_send())
    each_other(lambda d: vn_copy(d).wait_send())
    xh_copy.wait_send()
    each_other(lambda d: ag_copy(d).wait_send())
    for c in range(4):
        piece = gout.at[1 - core, :, 128 * c : 128 * c + 128, :]
        send(piece, piece, s_fin.at[c], r_fin.at[c], me, sib).wait_recv()
        leave(1 - core, c)
        fin_copy(c).wait_send()


def step_kernel(state, cot, w_in, w_out, gain, sb, cc, fa, fb, ter, ktab):
    adj, ycol, yrow, sel, spread = tables()
    vm = lambda *s, t=BF16: pltpu.VMEM(s, t)
    dma = lambda *s: pltpu.SemaphoreType.DMA(s)
    one = pltpu.SemaphoreType.DMA
    scratch = [
        vm(2, 2, 512, 512),
        vm(NS, CELLS), vm(CELLS, NS), vm(CELLS, NS), vm(NS, CH), vm(NS, CH), vm(NS, CH), vm(NS, CH),
        vm(PAIRS, 8, 128, t=F32), vm(NL, 8, 128, t=F32), vm(3, 8, 128, t=F32), vm(8, 8, 128, t=F32),
        vm(EXT, CH), vm(EXT, CH), vm(192, CH), vm(192, CH), vm(CELLS, CH), vm(CELLS, CH, t=F32),
        vm(EXT, EXT), vm(EXT, EXT), vm(EXT, EXT), vm(EXT, EXT),
        vm(EXT, CELLS), vm(EXT, CELLS), vm(CELLS, EXT), vm(CELLS, EXT),
        vm(CELLS, CH), vm(CELLS, HID, t=F32), vm(CELLS, HID),
        vm(2, 2, 512, 512), vm(2, 512, 512), vm(2, 512, 512), vm(NL, 2, 16, 512),
        vm(2, 16, 512, t=F32), vm(2, 16, 512, t=F32),
        vm(8, 128, t=F32), vm(NT, 8, 128, t=F32), vm(8, 128, t=F32), vm(NL, 8, 128, t=F32),
        dma(NL), dma(NL), dma(NL), dma(NL), dma(NL), dma(NL), dma(8), dma(8), dma(8), dma(8),
        dma(8), dma(8), dma(2), dma(2), dma(NL), dma(NL), one, one, dma(NL), dma(NL), dma(4), dma(4),
        dma(NT), dma(NT), dma(NL), dma(NL),
    ]
    vmem = pl.BlockSpec(memory_space=pltpu.VMEM)
    smem = pl.BlockSpec(memory_space=pltpu.SMEM)
    return pl.pallas_call(
        kernel,
        out_shape=(
            jax.ShapeDtypeStruct((CELLS, CH), BF16),
            jax.ShapeDtypeStruct((CELLS, CH), BF16),
            jax.ShapeDtypeStruct((CH, HID), BF16),
            jax.ShapeDtypeStruct((HID, CH), BF16),
            jax.ShapeDtypeStruct((1, CH), F32),
            jax.ShapeDtypeStruct((1, 1), F32),
        ),
        in_specs=[vmem] * 10 + [smem] + [vmem] * 5,
        out_specs=(vmem,) * 6,
        scratch_shapes=scratch,
        compiler_params=pltpu.CompilerParams(
            collective_id=0, has_side_effects=True, vmem_limit_bytes=60 * 1024 * 1024
        ),
        cost_estimate=pl.CostEstimate(
            flops=12 * 10**9, bytes_accessed=8 * 2**20, transcendentals=CELLS * HID
        ),
    )(
        state, cot, w_in, w_out, gain.reshape(1, CH), sb, cc, fa, fb, ter, ktab,
        jnp.asarray(adj, BF16), jnp.asarray(ycol, BF16), jnp.asarray(yrow, F32),
        jnp.asarray(sel, BF16), jnp.asarray(spread, F32),
    )


def on_device(*args):
    state, cot = (v.reshape(CELLS, CH) for v in args[:2])
    state_out, state_grad, inner, outer, gain, over = step_kernel(state, cot, *args[2:])
    over = over.reshape(())
    shape = (16, 16, CH)

    def general(*carry):
        made = on_device_general(*args)
        return (jnp.zeros_like(over), *(v.astype(BF16) for v in made[:4]), made[4])

    carry = (
        over, state_out.reshape(shape), state_grad.reshape(shape), inner, outer,
        gain.reshape(CH),
    )
    carry = lax.while_loop(lambda c: c[0] > 0.0, lambda c: general(*c), carry)
    return (carry[1], carry[2], carry[3].astype(F32), carry[4].astype(F32), carry[5])


def solution(mesh):
    placed = (
        P("lon", "lat", None),
        P("lon", "lat", None),
        P(),
        P(),
        P(),
        P("lon", "lat"),
        P("lon", "lat"),
        P("lon", "lat"),
        P("lon", "lat"),
        P("lon", "lat"),
        P(),
    )
    return jax.shard_map(
        on_device,
        mesh=mesh,
        in_specs=placed,
        out_specs=(P("lon", "lat", None), P("lon", "lat", None), P(), P(), P()),
        check_vma=False,
    )
```

```python
import functools

import jax
import jax.numpy as jnp
import numpy as np
from jax import lax
from jax.experimental import pallas as pl
from jax.experimental.pallas import tpu as pltpu
from jax.sharding import PartitionSpec as P

MESH = pl.DeviceIdType.MESH
F32 = jnp.float32
BF16 = jnp.bfloat16
NL = 32
NT = 4
CELLS = 256
CH = 512
HID = 1024
SLOT = 64
NS = NL * SLOT
PAIRS = NL // 2
NEAR_PAIRS = 7
CAPS = ((32, 32), (48, 16))
BACK = 6
EXT = 640
NEIGH = ((-1, 0), (1, 0), (0, -1), (0, 1), (-1, -1), (-1, 1), (1, -1), (1, 1))


def ext_cells():
    cells = [(x, y) for x in range(16) for y in range(16)]
    low, mid, top = range(-4, 0), range(16), range(16, 20)
    for dx, dy in NEIGH:
        xs = (low, mid, top)[dx + 1]
        ys = (low, mid, top)[dy + 1]
        cells += [(x, y) for x in xs for y in ys]
    return np.array(cells)


def tables():
    cells = ext_cells()
    count = len(cells)
    dist = np.abs(cells[:, None] - cells[None, :]).sum(-1)
    adj = np.zeros((EXT, EXT), np.float32)
    adj[:count, :count] = dist == 1
    ys = np.full((EXT,), -1000.0, np.float32)
    ys[:count] = cells[:, 1]
    ycol = np.broadcast_to(ys[:, None], (EXT, 128))
    yrow = ys[None, :]
    sel = np.zeros((384, CELLS), np.float32)
    at = 0
    for dx, dy in NEIGH:
        width = (4 if dx else 16) * (4 if dy else 16)
        for q in range(width):
            x, y = cells[256 + at + q]
            sel[at + q, (x - 16 * dx) * 16 + (y - 16 * dy)] = 1.0
        at += width
    spread = (np.arange(256)[None, :] % 16 == np.arange(16)[:, None]).astype(np.float32)
    return adj, ycol, yrow, sel, spread


def nn(a, b):
    return jnp.dot(a, b, preferred_element_type=F32)


def nt(a, b):
    return lax.dot_general(a, b, (((1,), (1,)), ((), ())), preferred_element_type=F32)


def tn(a, b):
    return lax.dot_general(a, b, (((0,), (0,)), ((), ())), preferred_element_type=F32)


def split2(v):
    hi = v.astype(BF16)
    return hi, (v - hi.astype(F32)).astype(BF16)


def iota(shape, dim):
    return lax.broadcasted_iota(jnp.int32, shape, dim).astype(F32)

STEPS = 4


def ring_pass(value, axis):
    size = lax.axis_size(axis)
    return lax.ppermute(value, axis, [(i, (i + 1) % size) for i in range(size)])


def ring_gather(value):
    size, me = lax.axis_size("lon"), lax.axis_index("lon")
    rows = value.shape[0]

    def step(k, carry):
        block, out = carry
        out = lax.dynamic_update_slice_in_dim(out, block, (me - k) % size * rows, 0)
        return ring_pass(block, "lon"), out

    out = jnp.zeros((size * rows,) + value.shape[1:], value.dtype)
    return lax.fori_loop(0, size, step, (value, out))[1]


def ring_scatter(value, rows):
    size, me = lax.axis_size("lon"), lax.axis_index("lon")

    def own(k):
        return lax.dynamic_slice_in_dim(value, (me + size - 1 - k) % size * rows, rows, 0)

    total = lax.fori_loop(1, size, lambda k, acc: ring_pass(acc, "lon") + own(k), own(0))
    return total.astype(jnp.bfloat16)


def ring_total(value):
    for repeat in range(2):
        for axis in ("lon", "lat"):
            def step(k, carry):
                block, total = carry
                block = ring_pass(block, axis)
                return block, total + block

            value = lax.fori_loop(1, lax.axis_size(axis), step, (value, value))[1]
        if repeat == 0:
            first = jnp.logical_and(lax.axis_index("lon") == 0, lax.axis_index("lat") == 0)
            value = jnp.where(first, value, 0.0)
    return value


def with_halo(value, sides, width, wrap):
    for axis, dim in sides:
        size, length = (lax.axis_size(axis), value.shape[dim])
        up = [(i, (i + 1) % size) for i in range(size if wrap else size - 1)]
        down = [(j, i) for i, j in up]
        last = lax.slice_in_dim(value, length - width, length, axis=dim)
        first = lax.slice_in_dim(value, 0, width, axis=dim)
        before = lax.ppermute(last, axis, up)
        after = lax.ppermute(first, axis, down)
        value = jnp.concatenate([before, value, after], axis=dim)
    return value


def flat_sources(source_block, corner_code, lat_cells):
    per_row = lat_cells // 8
    lon_part = source_block // per_row * 8 + corner_code // 8
    lat_part = source_block % per_row * 8 + corner_code % 8
    return lon_part * lat_cells + lat_part


def corner_table(flat_ids, frac_a, frac_b, lat_cells):
    shifted = jnp.stack([flat_ids, flat_ids + lat_cells, flat_ids + 1, flat_ids + lat_cells + 1])
    weights = jnp.stack(
        [
            (1.0 - frac_a) * (1.0 - frac_b),
            frac_a * (1.0 - frac_b),
            (1.0 - frac_a) * frac_b,
            frac_a * frac_b,
        ]
    )
    return (shifted, weights)


def laplace(field):
    wide = with_halo(field.astype(jnp.bfloat16), (("lon", 0),), 1, True).astype(field.dtype)
    tall = with_halo(field.astype(jnp.bfloat16), (("lat", 1),), 1, False).astype(field.dtype)
    return wide[2:] + wide[:-2] + tall[:, 2:] + tall[:, :-2] - 4.0 * field


def on_device_general(
    latent_state,
    cotangent,
    w_inner,
    w_outer,
    norm_gain,
    source_block,
    corner_code,
    frac_lon,
    frac_lat,
    terrain,
    kappa_table,
):
    lon_cells, lat_cells, chans = latent_state.shape
    cells = lon_cells * lat_cells
    flat_ids = flat_sources(source_block, corner_code, lat_cells)
    shifted, weights = corner_table(
        flat_ids.reshape(cells), frac_lon.reshape(cells), frac_lat.reshape(cells), lat_cells
    )
    shard_piece = ring_gather(latent_state)
    count = shard_piece.shape[0] * lat_cells
    local = shifted
    hits = local[:, :, None] == jnp.arange(count, dtype=jnp.int32)[None, None, :]
    select = jnp.sum(jnp.where(hits, weights[:, :, None], 0.0), 0)
    upper = select.astype(jnp.bfloat16)
    lower = (select - upper.astype(jnp.float32)).astype(jnp.bfloat16)
    values = shard_piece.reshape(count, chans)
    running = jnp.dot(upper, values, preferred_element_type=jnp.float32)
    drift = running + jnp.dot(lower, values, preferred_element_type=jnp.float32)
    drift = drift.reshape(lon_cells, lat_cells, chans)
    classes = jnp.arange(kappa_table.shape[0], dtype=jnp.int32)
    kappa = jnp.sum(jnp.where(terrain[..., None] == classes, kappa_table, 0.0), -1)[..., None]
    field = drift
    for turn_index in range(STEPS):
        field = field + kappa * laplace(field)
    flat_field = field.reshape(cells, chans)
    rstd = lax.rsqrt(jnp.mean(flat_field * flat_field, -1, keepdims=True) + 1e-06)
    normed = flat_field * rstd
    z_in = (normed * norm_gain).astype(jnp.bfloat16)
    pre_act = jnp.dot(z_in, w_inner, preferred_element_type=jnp.float32)
    act = jax.nn.silu(pre_act).astype(jnp.bfloat16)
    react = jnp.dot(act, w_outer, preferred_element_type=jnp.float32)
    state_out = (flat_field + react).astype(jnp.bfloat16).reshape(lon_cells, lat_cells, chans)
    cot = cotangent.reshape(cells, chans)
    local_outer = jnp.dot(act.T, cot, preferred_element_type=jnp.float32)
    grad_act = jnp.dot(cot, w_outer.T, preferred_element_type=jnp.float32)
    sigma = jax.nn.sigmoid(pre_act)
    grad_pre = (grad_act * sigma * (1.0 + pre_act * (1.0 - sigma))).astype(jnp.bfloat16)
    local_inner = jnp.dot(z_in.T, grad_pre, preferred_element_type=jnp.float32)
    grad_z = jnp.dot(grad_pre, w_inner.T, preferred_element_type=jnp.float32)
    local_gain = jnp.sum(grad_z * normed, 0)
    grad_norm = grad_z * norm_gain
    grad_field = cot.astype(jnp.float32) + rstd * (
        grad_norm - normed * jnp.mean(grad_norm * normed, -1, keepdims=True)
    )
    grad_field = grad_field.reshape(lon_cells, lat_cells, chans)
    for turn_index in range(STEPS):
        grad_field = grad_field + laplace(kappa * grad_field)
    grad_drift = grad_field.astype(jnp.bfloat16)
    parts = (weights[:, :, None] * grad_drift.reshape(cells, chans).astype(jnp.float32)).astype(
        jnp.bfloat16
    )
    count = lon_cells * lax.axis_size("lon")
    width = count * lat_cells
    local = shifted
    onehot = (local[:, :, None] == jnp.arange(width, dtype=jnp.int32)[None, None, :]).astype(
        jnp.bfloat16
    )
    term = jnp.einsum("ksr,ksc->rc", onehot, parts, preferred_element_type=jnp.float32)
    summed = ring_scatter(term.reshape(count, lat_cells, chans), lon_cells)
    grad_inner, grad_outer, grad_gain = (
        ring_total(v) for v in (local_inner, local_outer, local_gain)
    )
    return (state_out, summed, grad_inner, grad_outer, grad_gain)


def kernel(
    lat_state, cot_ref, w_in, w_out, gain_ref, sb_ref, cc_ref, fa_ref, fb_ref, ter_ref, ktab,
    adj_ref, ycol_ref, yrow_ref, sel_ref, spread_ref,
    out_ref, grad_ref, gi_ref, go_ref, gg_ref, over_ref,
    gout, G, W_hi, W_lo, rows_out, rows_in, gro, gin, req_out, req_in, t_out, t_in,
    ext_f, ext_b, stage_f, stage_b, gd_ref, Mh, Ml, M2h, M2l, Ah, Al, Bh, Bl,
    z_ref, slope_ref, gp_ref, gbuf, sib_in, hsum, rs_in, xh_out, xh_in, v_out, v_lat, v_sum, v_lon,
    s_req, r_req, s_row, r_row, s_gro, r_gro, s_ter, r_ter, s_hf, r_hf, s_hb, r_hb,
    s_sib, r_sib, s_rs, r_rs, s_xh, r_xh, s_ag, r_ag, s_fin, r_fin, s_vl, r_vl, s_vn, r_vn,
):
    me = lax.axis_index("lon")
    la = lax.axis_index("lat")
    core = lax.rem(la, 2)
    sib = la + 1 - 2 * core
    opp = lax.rem(la + 2, NT)

    inside = jnp.logical_and(la > 0, la < NT - 1)

    def sized(far, body):
        for kind, flag in ((0, jnp.logical_not(inside)), (1, inside)):
            @pl.when(flag)
            def _():
                body(CAPS[kind][far])

    def slot_sized(j, body):
        for far, flag in ((0, j < 2 * NEAR_PAIRS), (1, j >= 2 * NEAR_PAIRS)):
            @pl.when(jnp.logical_and(flag, j != BACK))
            def _():
                sized(far, body)

    def lon_at(d):
        return lax.rem(me + d + 2 * NL, NL)

    def lat_at(d):
        return lax.rem(la + d + NT, NT)

    def send(src, dst, ssem, rsem, lon, lat):
        return pltpu.make_async_remote_copy(
            src_ref=src, dst_ref=dst, send_sem=ssem, recv_sem=rsem,
            device_id=(lon, lat), device_id_type=MESH,
        )

    rows_in[...] = jnp.zeros((NS, CH), BF16)
    gin[...] = jnp.zeros((NS, CH), BF16)
    ext_f[576:EXT, :] = jnp.zeros((EXT - 576, CH), BF16)
    ext_b[576:EXT, :] = jnp.zeros((EXT - 576, CH), BF16)

    barrier = pltpu.get_barrier_semaphore()

    def greet(d, carry):
        pl.semaphore_signal(barrier, inc=1, device_id=(lon_at(d), la), device_id_type=MESH)
        return carry

    lax.fori_loop(1, NL, greet, 0)
    for dx, dy in NEIGH[2:]:
        pl.semaphore_signal(
            barrier, inc=1, device_id=(lon_at(dx), lat_at(dy)), device_id_type=MESH
        )
    pl.semaphore_signal(barrier, inc=1, device_id=(me, opp), device_id_type=MESH)

    raw = jnp.concatenate(
        [
            sb_ref[...].astype(F32), cc_ref[...].astype(F32), fa_ref[...], fb_ref[...],
            ter_ref[...].astype(F32),
        ],
        axis=0,
    )
    flat = jnp.dot(
        raw, spread_ref[...], precision=lax.Precision.HIGHEST, preferred_element_type=F32
    )
    own = jnp.floor(iota((16, CELLS), 1) * (1.0 / 16.0)) == iota((16, CELLS), 0)

    def line(k):
        return jnp.sum(jnp.where(own, flat[16 * k : 16 * k + 16], 0.0), 0, keepdims=True)

    sb, cc, fa, fb, ter = (line(k) for k in range(5))
    dev = jnp.floor(sb * 0.25)
    blon = jnp.floor(sb * 0.5)
    klon = jnp.floor(cc * 0.125)
    cell = ((blon - 2.0 * dev) * 8.0 + klon) * 16.0 + (sb - 2.0 * blon) * 8.0 + (cc - 8.0 * klon)
    slot = dev - me.astype(F32) + float(BACK)
    slot = jnp.where(slot < 0.0, slot + float(NL), slot)
    slot = jnp.where(slot >= float(NL), slot - float(NL), slot)
    hits = iota((NL, CELLS), 0) == slot
    before = (iota((CELLS, CELLS), 0) < iota((CELLS, CELLS), 1)).astype(F32).astype(BF16)
    counts = nn(jnp.where(hits, 1.0, 0.0).astype(BF16), before)
    rank = jnp.sum(jnp.where(hits, counts, 0.0), 0, keepdims=True)
    near_cap = jnp.where(inside, float(CAPS[1][0]), float(CAPS[0][0]))
    far_cap = jnp.where(inside, float(CAPS[1][1]), float(CAPS[0][1]))
    cap = jnp.where(slot < 2.0 * NEAR_PAIRS, near_cap, far_cap)
    fits = rank < cap
    place = jnp.where(fits, slot * float(SLOT) + rank, -1.0)
    over = jnp.sum(jnp.where(fits, 0.0, 1.0), axis=1, keepdims=True)

    def fill_g(q, carry):
        row = pl.multiple_of(q * 128, 128)
        at = iota((128, CELLS), 0) + lax.convert_element_type(row, F32)
        G[pl.ds(row, 128), :] = jnp.where(at == place, 1.0, 0.0).astype(BF16)
        return carry

    lax.fori_loop(0, PAIRS, fill_g, 0)

    def rows_of(lines, height, width):
        which = iota((height, width), 0)
        out = jnp.zeros((height, width), F32)
        for k, v in enumerate(lines):
            out = out + jnp.where(which == float(k), v, 0.0)
        return out

    fah = fa.astype(BF16).astype(F32)
    fam = (fa - fah).astype(BF16).astype(F32)
    fbh = fb.astype(BF16).astype(F32)
    fbm = (fb - fbh).astype(BF16).astype(F32)
    params = rows_of(
        [cell, fah, fam, fa - fah - fam, fbh, fbm, fb - fbh - fbm, jnp.ones_like(fa)], 16, CELLS
    ).astype(BF16)

    def fill_req(p, carry):
        req_out[p] = nt(params, G[pl.ds(pl.multiple_of(p * 128, 128), 128), :])[0:8]
        return carry

    lax.fori_loop(0, PAIRS, fill_req, 0)
    t_all = nt(jnp.broadcast_to(ter, (16, CELLS)).astype(BF16), sel_ref[...])
    for q in range(3):
        t_out[q] = t_all[0:8, 128 * q : 128 * q + 128]

    pl.semaphore_wait(barrier, NL - 1 + 7)

    def req_copy(j):
        return send(
            req_out.at[j // 2], req_in.at[j], s_req.at[j], r_req.at[j], lon_at(j - BACK), la
        )

    def each_pair(body):
        def step(j, carry):
            @pl.when(j != BACK)
            def _():
                body(j)

            return carry

        lax.fori_loop(0, NL, step, 0)

    each_pair(lambda j: req_copy(j).start())

    def ter_copy(n):
        dx, dy = NEIGH[n]
        tile = (0, 0, 1, 1, 2, 2, 2, 2)[n]
        return send(
            t_out.at[tile], t_in.at[n], s_ter.at[n], r_ter.at[n], lon_at(-dx), lat_at(-dy)
        )

    for n in range(8):
        ter_copy(n).start()
    req_in[BACK] = req_out[BACK // 2]

    each_pair(lambda j: req_copy(j).wait_recv())
    lane_low = iota((8, 128), 1) < float(SLOT)

    def row_copy(j, cap_j):
        at = pl.multiple_of(j * SLOT, SLOT)
        return send(
            rows_out.at[pl.ds(at, cap_j), :], rows_in.at[pl.ds(at, cap_j), :],
            s_row.at[j], r_row.at[j], lon_at(BACK - j), la,
        )

    def weigh(p):
        t = jnp.where(lane_low, req_in[2 * p], req_in[2 * p + 1])
        cid = t[0:1]
        a = t[1:2] + t[2:3] + t[3:4]
        b = t[4:5] + t[5:6] + t[6:7]
        real = t[7:8]
        at = iota((CELLS, 128), 0) - cid
        w = (
            jnp.where(at == 0.0, (1.0 - a) * (1.0 - b) * real, 0.0)
            + jnp.where(at == 16.0, a * (1.0 - b) * real, 0.0)
            + jnp.where(at == 1.0, (1.0 - a) * b * real, 0.0)
            + jnp.where(at == 17.0, a * b * real, 0.0)
        )
        col = pl.ds(pl.multiple_of(p * 128, 128), 128)
        W_hi[:, col], W_lo[:, col] = split2(w)

    def start_group(g, copy):
        def step(j, carry):
            slot_sized(j, lambda c: copy(j, c).start())
            return carry

        lax.fori_loop(8 * g, 8 * g + 8, step, 0)

    def make_rows(g, carry):
        for k in range(4):
            weigh(4 * g + k)
        part = pl.ds(pl.multiple_of(g * 512, 512), 512)
        v = lat_state[...]
        rows_out[part, :] = (tn(W_hi[:, part], v) + tn(W_lo[:, part], v)).astype(BF16)
        start_group(g, row_copy)
        return carry

    lax.fori_loop(0, 4, make_rows, 0)
    own_rows = slice(BACK * SLOT, BACK * SLOT + SLOT)
    rows_in[own_rows, :] = rows_out[own_rows, :]

    for n in range(8):
        ter_copy(n).wait_recv()
    lane = iota((8, 128), 1)
    quarter = jnp.floor(lane * (1.0 / 16.0))
    corner = t_in[4]
    for k in range(1, 4):
        corner = jnp.where(quarter == float(k), t_in[4 + k], corner)
    t_ext = jnp.concatenate(
        [
            jnp.broadcast_to(ter, (8, CELLS)),
            jnp.where(lane_low, t_in[0], t_in[1]),
            jnp.where(lane_low, t_in[2], t_in[3]),
            corner,
        ],
        axis=1,
    )
    lat0 = (la * 16).astype(F32)
    yr = yrow_ref[...] + lat0
    kap = jnp.zeros((8, EXT), F32)
    for k in range(8):
        kap = kap + jnp.where(t_ext == float(k), ktab[k], 0.0)
    kap = jnp.where((yr >= 0.0) & (yr < 64.0), kap[0:1], 0.0)
    def blocks(count, body):
        def step(q, carry):
            body(pl.ds(pl.multiple_of(q * 128, 128), 128), q * 128)
            return carry

        lax.fori_loop(0, count, step, 0)

    def fill_m(block, row):
        eye = iota((128, EXT), 0) + lax.convert_element_type(row, F32) == iota((128, EXT), 1)
        m = adj_ref[block, :].astype(F32) * kap + jnp.where(eye, 1.0 - 4.0 * kap, 0.0)
        yc = ycol_ref[block, 0:1].astype(F32) + lat0
        m = jnp.where((yc >= 0.0) & (yc < 64.0), m, 0.0)
        Mh[block, :], Ml[block, :] = split2(m)

    blocks(EXT // 128, fill_m)

    def prod(ah, al, bh, bl):
        return nn(ah, bh) + (nn(ah, bl) + nn(al, bh))

    def square(block, row):
        m2 = prod(Mh[block, :], Ml[block, :], Mh[...], Ml[...])
        M2h[block, :], M2l[block, :] = split2(m2)

    def last_a(block, row):
        v = prod(M2h[block, :], M2l[block, :], M2h[:, 0:CELLS], M2l[:, 0:CELLS])
        Ah[block, :], Al[block, :] = split2(v)

    def last_b(block, row):
        v = prod(M2h[block, :], M2l[block, :], M2h[...], M2l[...])
        Bh[block, :], Bl[block, :] = split2(v)

    blocks(EXT // 128, square)
    blocks(EXT // 128, last_a)
    blocks(CELLS // 128, last_b)

    def both_caps(body):
        def near(j, carry):
            @pl.when(j != BACK)
            def _():
                sized(0, lambda c: body(j, c))

            return carry

        def far(j, carry):
            sized(1, lambda c: body(j, c))
            return carry

        lax.fori_loop(0, 2 * NEAR_PAIRS, near, 0)
        lax.fori_loop(2 * NEAR_PAIRS, NL, far, 0)

    both_caps(lambda j, c: row_copy(j, c).wait_recv())
    ext_f[0:CELLS, :] = tn(G[...], rows_in[...]).astype(BF16)

    def halo_copy(ext, stage, ssem, rsem, n):
        dx, dy = NEIGH[n]
        start = (256, 320, 384, 448, 512, 528, 544, 560)[n]
        size = 64 if n < 4 else 16
        if n == 0:
            src = ext.at[192:256, :]
        elif n == 1:
            src = ext.at[0:64, :]
        else:
            src = stage.at[start - 384 : start - 384 + size, :]
        return send(
            src, ext.at[start : start + size, :], ssem.at[n], rsem.at[n], lon_at(-dx), lat_at(-dy)
        )

    def halo_start(ext, stage, ssem, rsem):
        for n in range(2):
            halo_copy(ext, stage, ssem, rsem, n).start()
        stage[...] = nn(sel_ref[128:320, :], ext[0:CELLS, :]).astype(BF16)
        for n in range(2, 8):
            halo_copy(ext, stage, ssem, rsem, n).start()

    halo_start(ext_f, stage_f, s_hf, r_hf)
    for n in range(8):
        halo_copy(ext_f, stage_f, s_hf, r_hf, n).wait_recv()
    field = tn(Ah[...], ext_f[...]) + tn(Al[...], ext_f[...])

    def sib_copy(k):
        return send(gbuf.at[1 - core, k], sib_in.at[k], s_sib.at[k], r_sib.at[k], me, sib)

    gain = gain_ref[...]
    r = lax.rsqrt(jnp.mean(field * field, axis=1, keepdims=True) + 1e-06)
    normed = field * r
    z_ref[...] = (normed * gain).astype(BF16)
    z = z_ref[...]
    cot = cot_ref[...]
    react = jnp.zeros((CELLS, CH), F32)
    for h in range(4):
        part = slice(256 * h, 256 * h + 256)
        p = nn(z, w_in[:, part])
        sig = 1.0 / (1.0 + jnp.exp(-p))
        act = (p * sig).astype(BF16)
        slope_ref[:, part] = sig * (1.0 + p * (1.0 - sig))
        half = slice(256 * (h % 2), 256 * (h % 2) + 256)
        gbuf[h // 2, 1, half, :] = tn(act, cot).astype(BF16)
        react = react + nn(act, w_out[part, :])
    sib_copy(1).start()
    out_ref[...] = (field + react).astype(BF16)
    gz = jnp.zeros((CELLS, CH), F32)
    for h in range(4):
        part = slice(256 * h, 256 * h + 256)
        gp = (nt(cot, w_out[part, :]) * slope_ref[:, part]).astype(BF16)
        gp_ref[:, part] = gp
        gz = gz + nt(gp, w_in[:, part])
    ggain = jnp.sum(gz * normed, axis=0, keepdims=True)
    gn = gz * gain
    gfield = cot.astype(F32) + r * (gn - normed * jnp.mean(gn * normed, axis=1, keepdims=True))
    g_hi, g_lo = split2(gfield)
    ext_b[0:CELLS, :] = g_hi
    halo_start(ext_b, stage_b, s_hb, r_hb)

    def inner_half(h, carry):
        half = pl.ds(pl.multiple_of(h * 512, 512), 512)
        gbuf[h, 0] = tn(z_ref[...], gp_ref[:, half]).astype(BF16)
        return carry

    lax.fori_loop(0, 2, inner_half, 0)
    sib_copy(0).start()
    v_out[...] = rows_of(
        [ggain[:, 128 * k : 128 * k + 128] for k in range(4)] + [jnp.broadcast_to(over, (1, 128))],
        8, 128,
    )

    def vl_copy(d):
        return send(v_out, v_lat.at[la], s_vl.at[d], r_vl.at[d], me, lat_at(d))

    for d in range(1, NT):
        vl_copy(d).start()
    v_lat[pl.ds(la, 1)] = v_out[...].reshape(1, 8, 128)

    def rs_copy(d):
        to = lon_at(d)
        return send(
            hsum.at[:, pl.ds(pl.multiple_of(to * 16, 16), 16), :], rs_in.at[d],
            s_rs.at[d], r_rs.at[d], to, la,
        )

    def each_other(body):
        def step(d, carry):
            body(d)
            return carry

        lax.fori_loop(1, NL, step, 0)

    for k in (1, 0):
        sib_copy(k).wait_recv()
        hsum[k] = (gbuf[core, k].astype(F32) + sib_in[k].astype(F32)).astype(BF16)
    each_other(lambda d: rs_copy(d).start())
    mine = pl.ds(pl.multiple_of(me * 16, 16), 16)
    rs_in[0] = hsum[:, mine, :]

    for n in range(8):
        halo_copy(ext_b, stage_b, s_hb, r_hb, n).wait_recv()
    gdrift = (
        nn(Bh[...], ext_b[...]) + nn(Bl[...], ext_b[...]) + nn(Bh[:, 0:CELLS], g_lo)
    ).astype(BF16)

    def gro_copy(j, cap_j):
        at = pl.multiple_of(j * SLOT, SLOT)
        return send(
            gro.at[pl.ds(at, cap_j), :], gin.at[pl.ds(at, cap_j), :],
            s_gro.at[j], r_gro.at[j], lon_at(j - BACK), la,
        )

    def bucket(g, carry):
        part = pl.ds(pl.multiple_of(g * 512, 512), 512)
        gro[part, :] = nn(G[part, :], gd_ref[...]).astype(BF16)
        start_group(g, gro_copy)
        return carry

    gd_ref[...] = gdrift
    lax.fori_loop(0, 4, bucket, 0)
    gin[own_rows, :] = gro[own_rows, :]

    for d in range(1, NT):
        vl_copy(d).wait_recv()
    v_sum[...] = v_lat[0] + v_lat[1] + v_lat[2] + v_lat[3]

    def vn_copy(d):
        return send(v_sum, v_lon.at[me], s_vn.at[d], r_vn.at[d], lon_at(d), la)

    each_other(lambda d: vn_copy(d).start())
    v_lon[pl.ds(me, 1)] = v_sum[...].reshape(1, 8, 128)

    each_other(lambda d: rs_copy(d).wait_recv())
    xh_out[...] = lax.fori_loop(
        0, NL, lambda d, acc: acc + rs_in[d].astype(F32), jnp.zeros((2, 16, CH), F32)
    )
    xh_copy = send(xh_out, xh_in, s_xh, r_xh, me, opp)
    xh_copy.start()
    xh_copy.wait_recv()
    gout[core, :, mine, :] = (xh_out[...] + xh_in[...]).astype(BF16)

    def ag_copy(d):
        piece = gout.at[core, :, mine, :]
        return send(piece, piece, s_ag.at[d], r_ag.at[me], lon_at(d), la)

    def ag_wait(q):
        piece = gout.at[core, :, pl.ds(pl.multiple_of(q * 16, 16), 16), :]
        send(piece, piece, s_ag.at[q], r_ag.at[q], q, la).wait_recv()

    each_other(lambda d: ag_copy(d).start())
    both_caps(lambda j, c: gro_copy(j, c).wait_recv())
    grad_ref[...] = (nn(W_hi[...], gin[...]) + nn(W_lo[...], gin[...])).astype(BF16)
    each_other(lambda d: vn_copy(d).wait_recv())
    total = v_lon[0]
    for k in range(1, NL):
        total = total + v_lon[k]
    for k in range(4):
        gg_ref[0:1, 128 * k : 128 * k + 128] = total[k : k + 1]
    over_ref[...] = total[4:5, 0:1]

    def fin_copy(c):
        piece = gout.at[core, :, 128 * c : 128 * c + 128, :]
        return send(piece, piece, s_fin.at[c], r_fin.at[c], me, sib)

    def leave(half, c):
        rows = slice(128 * c, 128 * c + 128)
        left = pl.ds(pl.multiple_of(half * 512, 512), 512)
        below = pl.ds(pl.multiple_of(half * 512 + 128 * c, 128), 128)
        gi_ref[rows, left] = gout[half, 0, rows, :]
        go_ref[below, :] = gout[half, 1, rows, :]

    for c in range(4):
        def arrive(q, carry):
            @pl.when(q != me)
            def _():
                ag_wait(q)

            return carry

        lax.fori_loop(8 * c, 8 * c + 8, arrive, 0)
        fin_copy(c).start()
        leave(core, c)

    each_pair(lambda j: req_copy(j).wait_send())
    for n in range(8):
        ter_copy(n).wait_send()
        halo_copy(ext_f, stage_f, s_hf, r_hf, n).wait_send()
        halo_copy(ext_b, stage_b, s_hb, r_hb, n).wait_send()
    both_caps(lambda j, c: row_copy(j, c).wait_send())
    both_caps(lambda j, c: gro_copy(j, c).wait_send())
    sib_copy(0).wait_send()
    sib_copy(1).wait_send()
    for d in range(1, NT):
        vl_copy(d).wait_send()
    each_other(lambda d: rs_copy(d).wait_send())
    each_other(lambda d: vn_copy(d).wait_send())
    xh_copy.wait_send()
    each_other(lambda d: ag_copy(d).wait_send())
    for c in range(4):
        piece = gout.at[1 - core, :, 128 * c : 128 * c + 128, :]
        send(piece, piece, s_fin.at[c], r_fin.at[c], me, sib).wait_recv()
        leave(1 - core, c)
        fin_copy(c).wait_send()


def step_kernel(state, cot, w_in, w_out, gain, sb, cc, fa, fb, ter, ktab):
    adj, ycol, yrow, sel, spread = tables()
    vm = lambda *s, t=BF16: pltpu.VMEM(s, t)
    dma = lambda *s: pltpu.SemaphoreType.DMA(s)
    one = pltpu.SemaphoreType.DMA
    scratch = [
        vm(2, 2, 512, 512),
        vm(NS, CELLS), vm(CELLS, NS), vm(CELLS, NS), vm(NS, CH), vm(NS, CH), vm(NS, CH), vm(NS, CH),
        vm(PAIRS, 8, 128, t=F32), vm(NL, 8, 128, t=F32), vm(3, 8, 128, t=F32), vm(8, 8, 128, t=F32),
        vm(EXT, CH), vm(EXT, CH), vm(192, CH), vm(192, CH), vm(CELLS, CH),
        vm(EXT, EXT), vm(EXT, EXT), vm(EXT, EXT), vm(EXT, EXT),
        vm(EXT, CELLS), vm(EXT, CELLS), vm(CELLS, EXT), vm(CELLS, EXT),
        vm(CELLS, CH), vm(CELLS, HID, t=F32), vm(CELLS, HID),
        vm(2, 2, 512, 512), vm(2, 512, 512), vm(2, 512, 512), vm(NL, 2, 16, 512),
        vm(2, 16, 512, t=F32), vm(2, 16, 512, t=F32),
        vm(8, 128, t=F32), vm(NT, 8, 128, t=F32), vm(8, 128, t=F32), vm(NL, 8, 128, t=F32),
        dma(NL), dma(NL), dma(NL), dma(NL), dma(NL), dma(NL), dma(8), dma(8), dma(8), dma(8),
        dma(8), dma(8), dma(2), dma(2), dma(NL), dma(NL), one, one, dma(NL), dma(NL), dma(4), dma(4),
        dma(NT), dma(NT), dma(NL), dma(NL),
    ]
    vmem = pl.BlockSpec(memory_space=pltpu.VMEM)
    smem = pl.BlockSpec(memory_space=pltpu.SMEM)
    return pl.pallas_call(
        kernel,
        out_shape=(
            jax.ShapeDtypeStruct((CELLS, CH), BF16),
            jax.ShapeDtypeStruct((CELLS, CH), BF16),
            jax.ShapeDtypeStruct((CH, HID), BF16),
            jax.ShapeDtypeStruct((HID, CH), BF16),
            jax.ShapeDtypeStruct((1, CH), F32),
            jax.ShapeDtypeStruct((1, 1), F32),
        ),
        in_specs=[vmem] * 10 + [smem] + [vmem] * 5,
        out_specs=(vmem,) * 6,
        scratch_shapes=scratch,
        compiler_params=pltpu.CompilerParams(
            collective_id=0, has_side_effects=True, vmem_limit_bytes=60 * 1024 * 1024
        ),
        cost_estimate=pl.CostEstimate(
            flops=12 * 10**9, bytes_accessed=8 * 2**20, transcendentals=CELLS * HID
        ),
    )(
        state, cot, w_in, w_out, gain.reshape(1, CH), sb, cc, fa, fb, ter, ktab,
        jnp.asarray(adj, BF16), jnp.asarray(ycol, BF16), jnp.asarray(yrow, F32),
        jnp.asarray(sel, BF16), jnp.asarray(spread, F32),
    )


def on_device(*args):
    state, cot = (v.reshape(CELLS, CH) for v in args[:2])
    state_out, state_grad, inner, outer, gain, over = step_kernel(state, cot, *args[2:])
    over = over.reshape(())
    shape = (16, 16, CH)

    def general(*carry):
        made = on_device_general(*args)
        return (jnp.zeros_like(over), *(v.astype(BF16) for v in made[:4]), made[4])

    carry = (
        over, state_out.reshape(shape), state_grad.reshape(shape), inner, outer,
        gain.reshape(CH),
    )
    carry = lax.while_loop(lambda c: c[0] > 0.0, lambda c: general(*c), carry)
    return (carry[1], carry[2], carry[3].astype(F32), carry[4].astype(F32), carry[5])


def solution(mesh):
    placed = (
        P("lon", "lat", None),
        P("lon", "lat", None),
        P(),
        P(),
        P(),
        P("lon", "lat"),
        P("lon", "lat"),
        P("lon", "lat"),
        P("lon", "lat"),
        P("lon", "lat"),
        P(),
    )
    return jax.shard_map(
        on_device,
        mesh=mesh,
        in_specs=placed,
        out_specs=(P("lon", "lat", None), P("lon", "lat", None), P(), P(), P()),
        check_vma=False,
    )
```

```python
import functools

import jax
import jax.numpy as jnp
import numpy as np
from jax import lax
from jax.experimental import pallas as pl
from jax.experimental.pallas import tpu as pltpu
from jax.sharding import PartitionSpec as P

MESH = pl.DeviceIdType.MESH
F32 = jnp.float32
BF16 = jnp.bfloat16
NL = 32
NT = 4
CELLS = 256
CH = 512
HID = 1024
SLOT = 64
NS = NL * SLOT
PAIRS = NL // 2
NEAR_PAIRS = 7
CAPS = ((32, 32), (48, 16))
BACK = 6
EXT = 640
NEIGH = ((-1, 0), (1, 0), (0, -1), (0, 1), (-1, -1), (-1, 1), (1, -1), (1, 1))


def ext_cells():
    cells = [(x, y) for x in range(16) for y in range(16)]
    low, mid, top = range(-4, 0), range(16), range(16, 20)
    for dx, dy in NEIGH:
        xs = (low, mid, top)[dx + 1]
        ys = (low, mid, top)[dy + 1]
        cells += [(x, y) for x in xs for y in ys]
    return np.array(cells)


def tables():
    cells = ext_cells()
    count = len(cells)
    dist = np.abs(cells[:, None] - cells[None, :]).sum(-1)
    adj = np.zeros((EXT, EXT), np.float32)
    adj[:count, :count] = dist == 1
    ys = np.full((EXT,), -1000.0, np.float32)
    ys[:count] = cells[:, 1]
    ycol = np.broadcast_to(ys[:, None], (EXT, 128))
    yrow = ys[None, :]
    sel = np.zeros((384, CELLS), np.float32)
    at = 0
    for dx, dy in NEIGH:
        width = (4 if dx else 16) * (4 if dy else 16)
        for q in range(width):
            x, y = cells[256 + at + q]
            sel[at + q, (x - 16 * dx) * 16 + (y - 16 * dy)] = 1.0
        at += width
    spread = (np.arange(256)[None, :] % 16 == np.arange(16)[:, None]).astype(np.float32)
    return adj, ycol, yrow, sel, spread


def nn(a, b):
    return jnp.dot(a, b, preferred_element_type=F32)


def nt(a, b):
    return lax.dot_general(a, b, (((1,), (1,)), ((), ())), preferred_element_type=F32)


def tn(a, b):
    return lax.dot_general(a, b, (((0,), (0,)), ((), ())), preferred_element_type=F32)


def split2(v):
    hi = v.astype(BF16)
    return hi, (v - hi.astype(F32)).astype(BF16)


def iota(shape, dim):
    return lax.broadcasted_iota(jnp.int32, shape, dim).astype(F32)

STEPS = 4


def ring_pass(value, axis):
    size = lax.axis_size(axis)
    return lax.ppermute(value, axis, [(i, (i + 1) % size) for i in range(size)])


def ring_gather(value):
    size, me = lax.axis_size("lon"), lax.axis_index("lon")
    rows = value.shape[0]

    def step(k, carry):
        block, out = carry
        out = lax.dynamic_update_slice_in_dim(out, block, (me - k) % size * rows, 0)
        return ring_pass(block, "lon"), out

    out = jnp.zeros((size * rows,) + value.shape[1:], value.dtype)
    return lax.fori_loop(0, size, step, (value, out))[1]


def ring_scatter(value, rows):
    size, me = lax.axis_size("lon"), lax.axis_index("lon")

    def own(k):
        return lax.dynamic_slice_in_dim(value, (me + size - 1 - k) % size * rows, rows, 0)

    total = lax.fori_loop(1, size, lambda k, acc: ring_pass(acc, "lon") + own(k), own(0))
    return total.astype(jnp.bfloat16)


def ring_total(value):
    for repeat in range(2):
        for axis in ("lon", "lat"):
            def step(k, carry):
                block, total = carry
                block = ring_pass(block, axis)
                return block, total + block

            value = lax.fori_loop(1, lax.axis_size(axis), step, (value, value))[1]
        if repeat == 0:
            first = jnp.logical_and(lax.axis_index("lon") == 0, lax.axis_index("lat") == 0)
            value = jnp.where(first, value, 0.0)
    return value


def with_halo(value, sides, width, wrap):
    for axis, dim in sides:
        size, length = (lax.axis_size(axis), value.shape[dim])
        up = [(i, (i + 1) % size) for i in range(size if wrap else size - 1)]
        down = [(j, i) for i, j in up]
        last = lax.slice_in_dim(value, length - width, length, axis=dim)
        first = lax.slice_in_dim(value, 0, width, axis=dim)
        before = lax.ppermute(last, axis, up)
        after = lax.ppermute(first, axis, down)
        value = jnp.concatenate([before, value, after], axis=dim)
    return value


def flat_sources(source_block, corner_code, lat_cells):
    per_row = lat_cells // 8
    lon_part = source_block // per_row * 8 + corner_code // 8
    lat_part = source_block % per_row * 8 + corner_code % 8
    return lon_part * lat_cells + lat_part


def corner_table(flat_ids, frac_a, frac_b, lat_cells):
    shifted = jnp.stack([flat_ids, flat_ids + lat_cells, flat_ids + 1, flat_ids + lat_cells + 1])
    weights = jnp.stack(
        [
            (1.0 - frac_a) * (1.0 - frac_b),
            frac_a * (1.0 - frac_b),
            (1.0 - frac_a) * frac_b,
            frac_a * frac_b,
        ]
    )
    return (shifted, weights)


def laplace(field):
    wide = with_halo(field.astype(jnp.bfloat16), (("lon", 0),), 1, True).astype(field.dtype)
    tall = with_halo(field.astype(jnp.bfloat16), (("lat", 1),), 1, False).astype(field.dtype)
    return wide[2:] + wide[:-2] + tall[:, 2:] + tall[:, :-2] - 4.0 * field


def on_device_general(
    latent_state,
    cotangent,
    w_inner,
    w_outer,
    norm_gain,
    source_block,
    corner_code,
    frac_lon,
    frac_lat,
    terrain,
    kappa_table,
):
    lon_cells, lat_cells, chans = latent_state.shape
    cells = lon_cells * lat_cells
    flat_ids = flat_sources(source_block, corner_code, lat_cells)
    shifted, weights = corner_table(
        flat_ids.reshape(cells), frac_lon.reshape(cells), frac_lat.reshape(cells), lat_cells
    )
    shard_piece = ring_gather(latent_state)
    count = shard_piece.shape[0] * lat_cells
    local = shifted
    hits = local[:, :, None] == jnp.arange(count, dtype=jnp.int32)[None, None, :]
    select = jnp.sum(jnp.where(hits, weights[:, :, None], 0.0), 0)
    upper = select.astype(jnp.bfloat16)
    lower = (select - upper.astype(jnp.float32)).astype(jnp.bfloat16)
    values = shard_piece.reshape(count, chans)
    running = jnp.dot(upper, values, preferred_element_type=jnp.float32)
    drift = running + jnp.dot(lower, values, preferred_element_type=jnp.float32)
    drift = drift.reshape(lon_cells, lat_cells, chans)
    classes = jnp.arange(kappa_table.shape[0], dtype=jnp.int32)
    kappa = jnp.sum(jnp.where(terrain[..., None] == classes, kappa_table, 0.0), -1)[..., None]
    field = drift
    for turn_index in range(STEPS):
        field = field + kappa * laplace(field)
    flat_field = field.reshape(cells, chans)
    rstd = lax.rsqrt(jnp.mean(flat_field * flat_field, -1, keepdims=True) + 1e-06)
    normed = flat_field * rstd
    z_in = (normed * norm_gain).astype(jnp.bfloat16)
    pre_act = jnp.dot(z_in, w_inner, preferred_element_type=jnp.float32)
    act = jax.nn.silu(pre_act).astype(jnp.bfloat16)
    react = jnp.dot(act, w_outer, preferred_element_type=jnp.float32)
    state_out = (flat_field + react).astype(jnp.bfloat16).reshape(lon_cells, lat_cells, chans)
    cot = cotangent.reshape(cells, chans)
    local_outer = jnp.dot(act.T, cot, preferred_element_type=jnp.float32)
    grad_act = jnp.dot(cot, w_outer.T, preferred_element_type=jnp.float32)
    sigma = jax.nn.sigmoid(pre_act)
    grad_pre = (grad_act * sigma * (1.0 + pre_act * (1.0 - sigma))).astype(jnp.bfloat16)
    local_inner = jnp.dot(z_in.T, grad_pre, preferred_element_type=jnp.float32)
    grad_z = jnp.dot(grad_pre, w_inner.T, preferred_element_type=jnp.float32)
    local_gain = jnp.sum(grad_z * normed, 0)
    grad_norm = grad_z * norm_gain
    grad_field = cot.astype(jnp.float32) + rstd * (
        grad_norm - normed * jnp.mean(grad_norm * normed, -1, keepdims=True)
    )
    grad_field = grad_field.reshape(lon_cells, lat_cells, chans)
    for turn_index in range(STEPS):
        grad_field = grad_field + laplace(kappa * grad_field)
    grad_drift = grad_field.astype(jnp.bfloat16)
    parts = (weights[:, :, None] * grad_drift.reshape(cells, chans).astype(jnp.float32)).astype(
        jnp.bfloat16
    )
    count = lon_cells * lax.axis_size("lon")
    width = count * lat_cells
    local = shifted
    onehot = (local[:, :, None] == jnp.arange(width, dtype=jnp.int32)[None, None, :]).astype(
        jnp.bfloat16
    )
    term = jnp.einsum("ksr,ksc->rc", onehot, parts, preferred_element_type=jnp.float32)
    summed = ring_scatter(term.reshape(count, lat_cells, chans), lon_cells)
    grad_inner, grad_outer, grad_gain = (
        ring_total(v) for v in (local_inner, local_outer, local_gain)
    )
    return (state_out, summed, grad_inner, grad_outer, grad_gain)


def kernel(
    lat_state, cot_ref, w_in, w_out, gain_ref, sb_ref, cc_ref, fa_ref, fb_ref, ter_ref, ktab,
    adj_ref, ycol_ref, yrow_ref, sel_ref, spread_ref,
    out_ref, grad_ref, gi_ref, go_ref, gg_ref, over_ref,
    gout, G, W_hi, W_lo, rows_out, rows_in, gro, gin, req_out, req_in, t_out, t_in,
    ext_f, ext_b, stage_f, stage_b, gd_ref, Mh, Ml, M2h, M2l, Ah, Al, Bh, Bl,
    z_ref, slope_ref, gp_ref, gbuf, sib_in, hsum, rs_in, xh_out, xh_in, v_out, v_lat, v_sum, v_lon,
    s_req, r_req, s_row, r_row, s_gro, r_gro, s_ter, r_ter, s_hf, r_hf, s_hb, r_hb,
    s_sib, r_sib, s_rs, r_rs, s_xh, r_xh, s_ag, r_ag, s_fin, r_fin, s_vl, r_vl, s_vn, r_vn,
):
    me = lax.axis_index("lon")
    la = lax.axis_index("lat")
    core = lax.rem(la, 2)
    sib = la + 1 - 2 * core
    opp = lax.rem(la + 2, NT)

    inside = jnp.logical_and(la > 0, la < NT - 1)

    def sized(far, body):
        for kind, flag in ((0, jnp.logical_not(inside)), (1, inside)):
            @pl.when(flag)
            def _():
                body(CAPS[kind][far])

    def slot_sized(j, body):
        for far, flag in ((0, j < 2 * NEAR_PAIRS), (1, j >= 2 * NEAR_PAIRS)):
            @pl.when(jnp.logical_and(flag, j != BACK))
            def _():
                sized(far, body)

    def lon_at(d):
        return lax.rem(me + d + 2 * NL, NL)

    def lat_at(d):
        return lax.rem(la + d + NT, NT)

    def send(src, dst, ssem, rsem, lon, lat):
        return pltpu.make_async_remote_copy(
            src_ref=src, dst_ref=dst, send_sem=ssem, recv_sem=rsem,
            device_id=(lon, lat), device_id_type=MESH,
        )

    rows_in[...] = jnp.zeros((NS, CH), BF16)
    gin[...] = jnp.zeros((NS, CH), BF16)
    ext_f[576:EXT, :] = jnp.zeros((EXT - 576, CH), BF16)
    ext_b[576:EXT, :] = jnp.zeros((EXT - 576, CH), BF16)

    barrier = pltpu.get_barrier_semaphore()

    def greet(d, carry):
        pl.semaphore_signal(barrier, inc=1, device_id=(lon_at(d), la), device_id_type=MESH)
        return carry

    lax.fori_loop(1, NL, greet, 0)
    for dx, dy in NEIGH[2:]:
        pl.semaphore_signal(
            barrier, inc=1, device_id=(lon_at(dx), lat_at(dy)), device_id_type=MESH
        )
    pl.semaphore_signal(barrier, inc=1, device_id=(me, opp), device_id_type=MESH)

    raw = jnp.concatenate(
        [
            sb_ref[...].astype(F32), cc_ref[...].astype(F32), fa_ref[...], fb_ref[...],
            ter_ref[...].astype(F32),
        ],
        axis=0,
    )
    flat = jnp.dot(
        raw, spread_ref[...], precision=lax.Precision.HIGHEST, preferred_element_type=F32
    )
    own = jnp.floor(iota((16, CELLS), 1) * (1.0 / 16.0)) == iota((16, CELLS), 0)

    def line(k):
        return jnp.sum(jnp.where(own, flat[16 * k : 16 * k + 16], 0.0), 0, keepdims=True)

    sb, cc, fa, fb, ter = (line(k) for k in range(5))
    dev = jnp.floor(sb * 0.25)
    blon = jnp.floor(sb * 0.5)
    klon = jnp.floor(cc * 0.125)
    cell = ((blon - 2.0 * dev) * 8.0 + klon) * 16.0 + (sb - 2.0 * blon) * 8.0 + (cc - 8.0 * klon)
    slot = dev - me.astype(F32) + float(BACK)
    slot = jnp.where(slot < 0.0, slot + float(NL), slot)
    slot = jnp.where(slot >= float(NL), slot - float(NL), slot)
    hits = iota((NL, CELLS), 0) == slot
    before = (iota((CELLS, CELLS), 0) < iota((CELLS, CELLS), 1)).astype(F32).astype(BF16)
    counts = nn(jnp.where(hits, 1.0, 0.0).astype(BF16), before)
    rank = jnp.sum(jnp.where(hits, counts, 0.0), 0, keepdims=True)
    near_cap = jnp.where(inside, float(CAPS[1][0]), float(CAPS[0][0]))
    far_cap = jnp.where(inside, float(CAPS[1][1]), float(CAPS[0][1]))
    cap = jnp.where(slot < 2.0 * NEAR_PAIRS, near_cap, far_cap)
    fits = rank < cap
    place = jnp.where(fits, slot * float(SLOT) + rank, -1.0)
    over = jnp.sum(jnp.where(fits, 0.0, 1.0), axis=1, keepdims=True)

    def fill_g(q, carry):
        row = pl.multiple_of(q * 128, 128)
        at = iota((128, CELLS), 0) + lax.convert_element_type(row, F32)
        G[pl.ds(row, 128), :] = jnp.where(at == place, 1.0, 0.0).astype(BF16)
        return carry

    lax.fori_loop(0, PAIRS, fill_g, 0)

    def rows_of(lines, height, width):
        which = iota((height, width), 0)
        out = jnp.zeros((height, width), F32)
        for k, v in enumerate(lines):
            out = out + jnp.where(which == float(k), v, 0.0)
        return out

    fah = fa.astype(BF16).astype(F32)
    fam = (fa - fah).astype(BF16).astype(F32)
    fbh = fb.astype(BF16).astype(F32)
    fbm = (fb - fbh).astype(BF16).astype(F32)
    params = rows_of(
        [cell, fah, fam, fa - fah - fam, fbh, fbm, fb - fbh - fbm, jnp.ones_like(fa)], 16, CELLS
    ).astype(BF16)

    def fill_req(p, carry):
        req_out[p] = nt(params, G[pl.ds(pl.multiple_of(p * 128, 128), 128), :])[0:8]
        return carry

    lax.fori_loop(0, PAIRS, fill_req, 0)
    t_all = nt(jnp.broadcast_to(ter, (16, CELLS)).astype(BF16), sel_ref[...])
    for q in range(3):
        t_out[q] = t_all[0:8, 128 * q : 128 * q + 128]

    pl.semaphore_wait(barrier, NL - 1 + 7)

    def req_copy(j):
        return send(
            req_out.at[j // 2], req_in.at[j], s_req.at[j], r_req.at[j], lon_at(j - BACK), la
        )

    def each_pair(body):
        def step(j, carry):
            @pl.when(j != BACK)
            def _():
                body(j)

            return carry

        lax.fori_loop(0, NL, step, 0)

    each_pair(lambda j: req_copy(j).start())

    def ter_copy(n):
        dx, dy = NEIGH[n]
        tile = (0, 0, 1, 1, 2, 2, 2, 2)[n]
        return send(
            t_out.at[tile], t_in.at[n], s_ter.at[n], r_ter.at[n], lon_at(-dx), lat_at(-dy)
        )

    for n in range(8):
        ter_copy(n).start()
    req_in[BACK] = req_out[BACK // 2]

    each_pair(lambda j: req_copy(j).wait_recv())
    lane_low = iota((8, 128), 1) < float(SLOT)

    def row_copy(j, cap_j):
        at = pl.multiple_of(j * SLOT, SLOT)
        return send(
            rows_out.at[pl.ds(at, cap_j), :], rows_in.at[pl.ds(at, cap_j), :],
            s_row.at[j], r_row.at[j], lon_at(BACK - j), la,
        )

    def weigh(p):
        t = jnp.where(lane_low, req_in[2 * p], req_in[2 * p + 1])
        cid = t[0:1]
        a = t[1:2] + t[2:3] + t[3:4]
        b = t[4:5] + t[5:6] + t[6:7]
        real = t[7:8]
        at = iota((CELLS, 128), 0) - cid
        w = (
            jnp.where(at == 0.0, (1.0 - a) * (1.0 - b) * real, 0.0)
            + jnp.where(at == 16.0, a * (1.0 - b) * real, 0.0)
            + jnp.where(at == 1.0, (1.0 - a) * b * real, 0.0)
            + jnp.where(at == 17.0, a * b * real, 0.0)
        )
        col = pl.ds(pl.multiple_of(p * 128, 128), 128)
        W_hi[:, col], W_lo[:, col] = split2(w)

    def start_group(g, copy):
        def step(j, carry):
            slot_sized(j, lambda c: copy(j, c).start())
            return carry

        lax.fori_loop(8 * g, 8 * g + 8, step, 0)

    def make_rows(g, carry):
        for k in range(4):
            weigh(4 * g + k)
        part = pl.ds(pl.multiple_of(g * 512, 512), 512)
        v = lat_state[...]
        rows_out[part, :] = (tn(W_hi[:, part], v) + tn(W_lo[:, part], v)).astype(BF16)
        start_group(g, row_copy)
        return carry

    lax.fori_loop(0, 4, make_rows, 0)
    own_rows = slice(BACK * SLOT, BACK * SLOT + SLOT)
    rows_in[own_rows, :] = rows_out[own_rows, :]

    for n in range(8):
        ter_copy(n).wait_recv()
    lane = iota((8, 128), 1)
    quarter = jnp.floor(lane * (1.0 / 16.0))
    corner = t_in[4]
    for k in range(1, 4):
        corner = jnp.where(quarter == float(k), t_in[4 + k], corner)
    t_ext = jnp.concatenate(
        [
            jnp.broadcast_to(ter, (8, CELLS)),
            jnp.where(lane_low, t_in[0], t_in[1]),
            jnp.where(lane_low, t_in[2], t_in[3]),
            corner,
        ],
        axis=1,
    )
    lat0 = (la * 16).astype(F32)
    yr = yrow_ref[...] + lat0
    kap = jnp.zeros((8, EXT), F32)
    for k in range(8):
        kap = kap + jnp.where(t_ext == float(k), ktab[k], 0.0)
    kap = jnp.where((yr >= 0.0) & (yr < 64.0), kap[0:1], 0.0)
    def blocks(count, body):
        def step(q, carry):
            body(pl.ds(pl.multiple_of(q * 128, 128), 128), q * 128)
            return carry

        lax.fori_loop(0, count, step, 0)

    def fill_m(block, row):
        eye = iota((128, EXT), 0) + lax.convert_element_type(row, F32) == iota((128, EXT), 1)
        m = adj_ref[block, :].astype(F32) * kap + jnp.where(eye, 1.0 - 4.0 * kap, 0.0)
        yc = ycol_ref[block, 0:1].astype(F32) + lat0
        m = jnp.where((yc >= 0.0) & (yc < 64.0), m, 0.0)
        Mh[block, :], Ml[block, :] = split2(m)

    blocks(EXT // 128, fill_m)

    def prod(ah, al, bh, bl):
        return nn(ah, bh) + (nn(ah, bl) + nn(al, bh))

    def square(block, row):
        m2 = prod(Mh[block, :], Ml[block, :], Mh[...], Ml[...])
        M2h[block, :], M2l[block, :] = split2(m2)

    def last_a(block, row):
        v = prod(M2h[block, :], M2l[block, :], M2h[:, 0:CELLS], M2l[:, 0:CELLS])
        Ah[block, :], Al[block, :] = split2(v)

    def last_b(block, row):
        v = prod(M2h[block, :], M2l[block, :], M2h[...], M2l[...])
        Bh[block, :], Bl[block, :] = split2(v)

    blocks(EXT // 128, square)
    blocks(EXT // 128, last_a)
    blocks(CELLS // 128, last_b)

    def both_caps(body):
        def near(j, carry):
            @pl.when(j != BACK)
            def _():
                sized(0, lambda c: body(j, c))

            return carry

        def far(j, carry):
            sized(1, lambda c: body(j, c))
            return carry

        lax.fori_loop(0, 2 * NEAR_PAIRS, near, 0)
        lax.fori_loop(2 * NEAR_PAIRS, NL, far, 0)

    both_caps(lambda j, c: row_copy(j, c).wait_recv())
    ext_f[0:CELLS, :] = tn(G[...], rows_in[...]).astype(BF16)

    def halo_copy(ext, stage, ssem, rsem, n):
        dx, dy = NEIGH[n]
        start = (256, 320, 384, 448, 512, 528, 544, 560)[n]
        size = 64 if n < 4 else 16
        if n == 0:
            src = ext.at[192:256, :]
        elif n == 1:
            src = ext.at[0:64, :]
        else:
            src = stage.at[start - 384 : start - 384 + size, :]
        return send(
            src, ext.at[start : start + size, :], ssem.at[n], rsem.at[n], lon_at(-dx), lat_at(-dy)
        )

    def halo_start(ext, stage, ssem, rsem):
        stage[...] = nn(sel_ref[128:320, :], ext[0:CELLS, :]).astype(BF16)
        for n in (2, 3, 4, 5, 6, 7, 0, 1):
            halo_copy(ext, stage, ssem, rsem, n).start()

    halo_start(ext_f, stage_f, s_hf, r_hf)
    for n in range(8):
        halo_copy(ext_f, stage_f, s_hf, r_hf, n).wait_recv()
    field = tn(Ah[...], ext_f[...]) + tn(Al[...], ext_f[...])

    def sib_copy(k):
        return send(gbuf.at[1 - core, k], sib_in.at[k], s_sib.at[k], r_sib.at[k], me, sib)

    gain = gain_ref[...]
    r = lax.rsqrt(jnp.mean(field * field, axis=1, keepdims=True) + 1e-06)
    normed = field * r
    z_ref[...] = (normed * gain).astype(BF16)
    z = z_ref[...]
    cot = cot_ref[...]
    react = jnp.zeros((CELLS, CH), F32)
    for h in range(4):
        part = slice(256 * h, 256 * h + 256)
        p = nn(z, w_in[:, part])
        sig = 1.0 / (1.0 + jnp.exp(-p))
        act = (p * sig).astype(BF16)
        slope_ref[:, part] = sig * (1.0 + p * (1.0 - sig))
        half = slice(256 * (h % 2), 256 * (h % 2) + 256)
        gbuf[h // 2, 1, half, :] = tn(act, cot).astype(BF16)
        react = react + nn(act, w_out[part, :])
    sib_copy(1).start()
    out_ref[...] = (field + react).astype(BF16)
    gz = jnp.zeros((CELLS, CH), F32)
    for h in range(4):
        part = slice(256 * h, 256 * h + 256)
        gp = (nt(cot, w_out[part, :]) * slope_ref[:, part]).astype(BF16)
        gp_ref[:, part] = gp
        gz = gz + nt(gp, w_in[:, part])
    ggain = jnp.sum(gz * normed, axis=0, keepdims=True)
    gn = gz * gain
    gfield = cot.astype(F32) + r * (gn - normed * jnp.mean(gn * normed, axis=1, keepdims=True))
    g_hi, g_lo = split2(gfield)
    ext_b[0:CELLS, :] = g_hi
    halo_start(ext_b, stage_b, s_hb, r_hb)

    def inner_half(h, carry):
        half = pl.ds(pl.multiple_of(h * 512, 512), 512)
        gbuf[h, 0] = tn(z_ref[...], gp_ref[:, half]).astype(BF16)
        return carry

    lax.fori_loop(0, 2, inner_half, 0)
    sib_copy(0).start()
    v_out[...] = rows_of(
        [ggain[:, 128 * k : 128 * k + 128] for k in range(4)] + [jnp.broadcast_to(over, (1, 128))],
        8, 128,
    )

    def vl_copy(d):
        return send(v_out, v_lat.at[la], s_vl.at[d], r_vl.at[d], me, lat_at(d))

    for d in range(1, NT):
        vl_copy(d).start()
    v_lat[pl.ds(la, 1)] = v_out[...].reshape(1, 8, 128)

    def rs_copy(d):
        to = lon_at(d)
        return send(
            hsum.at[:, pl.ds(pl.multiple_of(to * 16, 16), 16), :], rs_in.at[d],
            s_rs.at[d], r_rs.at[d], to, la,
        )

    def each_other(body):
        def step(d, carry):
            body(d)
            return carry

        lax.fori_loop(1, NL, step, 0)

    for k in (1, 0):
        sib_copy(k).wait_recv()
        hsum[k] = (gbuf[core, k].astype(F32) + sib_in[k].astype(F32)).astype(BF16)
    each_other(lambda d: rs_copy(d).start())
    mine = pl.ds(pl.multiple_of(me * 16, 16), 16)
    rs_in[0] = hsum[:, mine, :]

    for n in range(8):
        halo_copy(ext_b, stage_b, s_hb, r_hb, n).wait_recv()
    gdrift = (
        nn(Bh[...], ext_b[...]) + nn(Bl[...], ext_b[...]) + nn(Bh[:, 0:CELLS], g_lo)
    ).astype(BF16)

    def gro_copy(j, cap_j):
        at = pl.multiple_of(j * SLOT, SLOT)
        return send(
            gro.at[pl.ds(at, cap_j), :], gin.at[pl.ds(at, cap_j), :],
            s_gro.at[j], r_gro.at[j], lon_at(j - BACK), la,
        )

    def bucket(g, carry):
        part = pl.ds(pl.multiple_of(g * 512, 512), 512)
        gro[part, :] = nn(G[part, :], gd_ref[...]).astype(BF16)
        start_group(g, gro_copy)
        return carry

    gd_ref[...] = gdrift
    lax.fori_loop(0, 4, bucket, 0)
    gin[own_rows, :] = gro[own_rows, :]

    for d in range(1, NT):
        vl_copy(d).wait_recv()
    v_sum[...] = v_lat[0] + v_lat[1] + v_lat[2] + v_lat[3]

    def vn_copy(d):
        return send(v_sum, v_lon.at[me], s_vn.at[d], r_vn.at[d], lon_at(d), la)

    each_other(lambda d: vn_copy(d).start())
    v_lon[pl.ds(me, 1)] = v_sum[...].reshape(1, 8, 128)

    each_other(lambda d: rs_copy(d).wait_recv())
    xh_out[...] = lax.fori_loop(
        0, NL, lambda d, acc: acc + rs_in[d].astype(F32), jnp.zeros((2, 16, CH), F32)
    )
    xh_copy = send(xh_out, xh_in, s_xh, r_xh, me, opp)
    xh_copy.start()
    xh_copy.wait_recv()
    gout[core, :, mine, :] = (xh_out[...] + xh_in[...]).astype(BF16)

    def ag_copy(d):
        piece = gout.at[core, :, mine, :]
        return send(piece, piece, s_ag.at[d], r_ag.at[me], lon_at(d), la)

    def ag_wait(q):
        piece = gout.at[core, :, pl.ds(pl.multiple_of(q * 16, 16), 16), :]
        send(piece, piece, s_ag.at[q], r_ag.at[q], q, la).wait_recv()

    each_other(lambda d: ag_copy(d).start())
    both_caps(lambda j, c: gro_copy(j, c).wait_recv())
    grad_ref[...] = (nn(W_hi[...], gin[...]) + nn(W_lo[...], gin[...])).astype(BF16)
    each_other(lambda d: vn_copy(d).wait_recv())
    total = v_lon[0]
    for k in range(1, NL):
        total = total + v_lon[k]
    for k in range(4):
        gg_ref[0:1, 128 * k : 128 * k + 128] = total[k : k + 1]
    over_ref[...] = total[4:5, 0:1]

    def fin_copy(c):
        piece = gout.at[core, :, 128 * c : 128 * c + 128, :]
        return send(piece, piece, s_fin.at[c], r_fin.at[c], me, sib)

    def leave(half, c):
        rows = slice(128 * c, 128 * c + 128)
        left = pl.ds(pl.multiple_of(half * 512, 512), 512)
        below = pl.ds(pl.multiple_of(half * 512 + 128 * c, 128), 128)
        gi_ref[rows, left] = gout[half, 0, rows, :]
        go_ref[below, :] = gout[half, 1, rows, :]

    for c in range(4):
        def arrive(q, carry):
            @pl.when(q != me)
            def _():
                ag_wait(q)

            return carry

        lax.fori_loop(8 * c, 8 * c + 8, arrive, 0)
        fin_copy(c).start()
        leave(core, c)

    each_pair(lambda j: req_copy(j).wait_send())
    for n in range(8):
        ter_copy(n).wait_send()
        halo_copy(ext_f, stage_f, s_hf, r_hf, n).wait_send()
        halo_copy(ext_b, stage_b, s_hb, r_hb, n).wait_send()
    both_caps(lambda j, c: row_copy(j, c).wait_send())
    both_caps(lambda j, c: gro_copy(j, c).wait_send())
    sib_copy(0).wait_send()
    sib_copy(1).wait_send()
    for d in range(1, NT):
        vl_copy(d).wait_send()
    each_other(lambda d: rs_copy(d).wait_send())
    each_other(lambda d: vn_copy(d).wait_send())
    xh_copy.wait_send()
    each_other(lambda d: ag_copy(d).wait_send())
    for c in range(4):
        piece = gout.at[1 - core, :, 128 * c : 128 * c + 128, :]
        send(piece, piece, s_fin.at[c], r_fin.at[c], me, sib).wait_recv()
        leave(1 - core, c)
        fin_copy(c).wait_send()


def step_kernel(state, cot, w_in, w_out, gain, sb, cc, fa, fb, ter, ktab):
    adj, ycol, yrow, sel, spread = tables()
    vm = lambda *s, t=BF16: pltpu.VMEM(s, t)
    dma = lambda *s: pltpu.SemaphoreType.DMA(s)
    one = pltpu.SemaphoreType.DMA
    scratch = [
        vm(2, 2, 512, 512),
        vm(NS, CELLS), vm(CELLS, NS), vm(CELLS, NS), vm(NS, CH), vm(NS, CH), vm(NS, CH), vm(NS, CH),
        vm(PAIRS, 8, 128, t=F32), vm(NL, 8, 128, t=F32), vm(3, 8, 128, t=F32), vm(8, 8, 128, t=F32),
        vm(EXT, CH), vm(EXT, CH), vm(192, CH), vm(192, CH), vm(CELLS, CH),
        vm(EXT, EXT), vm(EXT, EXT), vm(EXT, EXT), vm(EXT, EXT),
        vm(EXT, CELLS), vm(EXT, CELLS), vm(CELLS, EXT), vm(CELLS, EXT),
        vm(CELLS, CH), vm(CELLS, HID, t=F32), vm(CELLS, HID),
        vm(2, 2, 512, 512), vm(2, 512, 512), vm(2, 512, 512), vm(NL, 2, 16, 512),
        vm(2, 16, 512, t=F32), vm(2, 16, 512, t=F32),
        vm(8, 128, t=F32), vm(NT, 8, 128, t=F32), vm(8, 128, t=F32), vm(NL, 8, 128, t=F32),
        dma(NL), dma(NL), dma(NL), dma(NL), dma(NL), dma(NL), dma(8), dma(8), dma(8), dma(8),
        dma(8), dma(8), dma(2), dma(2), dma(NL), dma(NL), one, one, dma(NL), dma(NL), dma(4), dma(4),
        dma(NT), dma(NT), dma(NL), dma(NL),
    ]
    vmem = pl.BlockSpec(memory_space=pltpu.VMEM)
    smem = pl.BlockSpec(memory_space=pltpu.SMEM)
    return pl.pallas_call(
        kernel,
        out_shape=(
            jax.ShapeDtypeStruct((CELLS, CH), BF16),
            jax.ShapeDtypeStruct((CELLS, CH), BF16),
            jax.ShapeDtypeStruct((CH, HID), BF16),
            jax.ShapeDtypeStruct((HID, CH), BF16),
            jax.ShapeDtypeStruct((1, CH), F32),
            jax.ShapeDtypeStruct((1, 1), F32),
        ),
        in_specs=[vmem] * 10 + [smem] + [vmem] * 5,
        out_specs=(vmem,) * 6,
        scratch_shapes=scratch,
        compiler_params=pltpu.CompilerParams(
            collective_id=0, has_side_effects=True, vmem_limit_bytes=60 * 1024 * 1024
        ),
        cost_estimate=pl.CostEstimate(
            flops=12 * 10**9, bytes_accessed=8 * 2**20, transcendentals=CELLS * HID
        ),
    )(
        state, cot, w_in, w_out, gain.reshape(1, CH), sb, cc, fa, fb, ter, ktab,
        jnp.asarray(adj, BF16), jnp.asarray(ycol, BF16), jnp.asarray(yrow, F32),
        jnp.asarray(sel, BF16), jnp.asarray(spread, F32),
    )


def on_device(*args):
    state, cot = (v.reshape(CELLS, CH) for v in args[:2])
    state_out, state_grad, inner, outer, gain, over = step_kernel(state, cot, *args[2:])
    over = over.reshape(())
    shape = (16, 16, CH)

    def general(*carry):
        made = on_device_general(*args)
        return (jnp.zeros_like(over), *(v.astype(BF16) for v in made[:4]), made[4])

    carry = (
        over, state_out.reshape(shape), state_grad.reshape(shape), inner, outer,
        gain.reshape(CH),
    )
    carry = lax.while_loop(lambda c: c[0] > 0.0, lambda c: general(*c), carry)
    return (carry[1], carry[2], carry[3].astype(F32), carry[4].astype(F32), carry[5])


def solution(mesh):
    placed = (
        P("lon", "lat", None),
        P("lon", "lat", None),
        P(),
        P(),
        P(),
        P("lon", "lat"),
        P("lon", "lat"),
        P("lon", "lat"),
        P("lon", "lat"),
        P("lon", "lat"),
        P(),
    )
    return jax.shard_map(
        on_device,
        mesh=mesh,
        in_specs=placed,
        out_specs=(P("lon", "lat", None), P("lon", "lat", None), P(), P(), P()),
        check_vma=False,
    )
```
